512 devices in a mesh: frames: 32 (over x, y_lo, core), labels: 16 (over z, y_hi).
Axes of the slice: x: 4, y: 8 (y_hi: 2, y_lo: 4; y = y_hi * 4 + y_lo), z: 8, core: 2. Of those that a mesh axis runs over, the one named last changes fastest.
Arguments:
- encoder_out: bfloat16 [3072, 640], P('frames'), may hold values from -6 to 6
- predictor_out: bfloat16 [256, 640], P('labels'), may hold values from -6 to 6
- out_weight: bfloat16 [640, 1024], replicated, may hold values from -0.25 to 0.25
- out_bias: float32 [1024], replicated, may hold values from -4 to 4
- target_labels: int32 [256], P('labels'), may hold values from 1 to 1023
- lengths: int32 [2], replicated, may hold values from 1 to 3072, as said below
- alpha_saved: float32 [3072, 256], P('frames', 'labels')
- beta_saved: float32 [3072, 256], P('frames', 'labels')
- log_likelihood: float32 [1], replicated, may hold values from -839.5 to -838.5
Outputs:
- grad_encoder: float32 [3072, 640], P('frames', 'labels')
- grad_predictor: float32 [256, 640], P('labels', 'frames')
- grad_weight: float32 [640, 1024], replicated
- grad_bias: float32 [1024], replicated
The draws below stay inside these ranges and needn't reach their ends.
Inputs may be any that keep to these rules, and one draw needn't show every extreme that they name: `lengths`: the frame length is 3072 and the label length lies in 240 to 255.
All inputs are finite; a program needn't handle non-finite values.
Results may differ from the reference program's by a relative error of at most 0.0034.
Values sent between devices are 32-bit elements; how exact they have to be, the bound alone decides.
A program may use at most 64 MiB of HBM per device.

```python
import jax
import jax.numpy as jnp
from jax import lax

H = 640
V = 1024
FR_DEV = 96
LB_DEV = 16
FRAMES = 3072
LABELS = 256


def draw_lengths(key, part):
    key = jax.random.fold_in(key, 5)
    label_len = jax.random.randint(key, (), LABELS - LB_DEV, LABELS)
    frame_len = jnp.array(FRAMES, jnp.int32)
    return jnp.stack([frame_len, label_len]).astype(jnp.int32)


def lattice_noise(key, low, high):
    return jax.random.uniform(key, (FRAMES, LABELS), jnp.float32, low, high)


def draw_alpha_saved(key, part):
    key = jax.random.fold_in(key, 1)
    frame_pos = jnp.arange(FRAMES, dtype=jnp.float32)[:, None]
    label_pos = jnp.arange(LABELS, dtype=jnp.float32)[None, :]
    noise = lattice_noise(key, -1.0, 0.5)
    return -0.25 * (frame_pos + label_pos) + noise


def draw_beta_saved(key, part):
    key = jax.random.fold_in(key, 2)
    frame_pos = jnp.arange(FRAMES, dtype=jnp.float32)[:, None]
    label_pos = jnp.arange(LABELS, dtype=jnp.float32)[None, :]
    noise = lattice_noise(key, -1.0, 0.5)
    return -0.25 * (FRAMES + LABELS - frame_pos - label_pos) + noise


def place_ends(result, key, smallest, top_value):
    extent = result.shape
    place = [jax.random.randint(jax.random.fold_in(key, axis), (), 0, extent[axis]) for axis in range(len(extent))]
    result = result.at[tuple(place)].set(smallest)
    longest = extent.index(max(extent))
    place[longest] = (place[longest] + 1) % extent[longest]
    return result.at[tuple(place)].set(top_value)


def shard_levels(key, dims, pieces, smallest, largest):
    loudness = 1.0
    for dim, blocks in pieces:
        draws = jax.random.uniform(jax.random.fold_in(jax.random.fold_in(key, 6), dim), (blocks,), jnp.float32, smallest / len(pieces), largest / len(pieces))
        loudness = loudness * jnp.repeat(jnp.exp(draws), dims[dim] // blocks).reshape((-1,) + (1,) * (len(dims) - 1 - dim))
    return loudness


def scatter_about(stream_key, dims, deviation, bound, pieces=(), kind=jnp.bfloat16):
    entries = jax.random.normal(stream_key, dims, jnp.float32) * deviation
    if len(pieces) > 0:
        entries = shard_levels(stream_key, dims, pieces, -0.22, 0.18) * entries
    return jnp.clip(entries, min=-bound, max=bound).astype(kind)


def setup_inputs(seed: int = 0) -> dict:
    streams_of = jax.random.split(jax.random.key(seed), 10)
    return {
        "encoder_out": scatter_about(streams_of[0], (FRAMES, H), 1.0, 6.0, ((0, 32),)),
        "predictor_out": scatter_about(streams_of[1], (LABELS, H), 1.0, 6.0, ((0, 16),)),
        "out_weight": scatter_about(streams_of[2], (H, V), H ** -0.5, 0.25),
        "out_bias": scatter_about(streams_of[3], (V,), 1.0, 4.0, (), jnp.float32),
        "target_labels": place_ends(jax.random.randint(streams_of[4], (LABELS,), 1, V), jax.random.fold_in(streams_of[4], 1), 1, V - 1).astype(jnp.int32),
        "lengths": draw_lengths(jax.random.fold_in(streams_of[9], 71), 0),
        "alpha_saved": draw_alpha_saved(jax.random.fold_in(streams_of[9], 71), 0),
        "beta_saved": draw_beta_saved(jax.random.fold_in(streams_of[9], 71), 0),
        "log_likelihood": jnp.clip(jax.random.uniform(streams_of[8], (1,), jnp.float32, -839.5, -838.5), -839.5, -838.5),
    }


def reference(encoder_out, predictor_out, out_weight, out_bias, target_labels, lengths, alpha_saved, beta_saved, log_likelihood):
    frame_len = lengths[0]
    label_len = lengths[1]
    log_total = log_likelihood[0]
    beta_frame = jnp.concatenate([beta_saved[1:], jnp.zeros((1, LABELS), jnp.float32)], axis=0)
    beta_label = jnp.concatenate([beta_saved[:, 1:], jnp.zeros((FRAMES, 1), jnp.float32)], axis=1)
    vocab_ids = jnp.arange(V, dtype=jnp.int32)
    label_hot = (target_labels[:, None] == vocab_ids[None, :]).astype(jnp.float32)
    blank_hot = (vocab_ids == 0).astype(jnp.float32)
    pred_f = predictor_out.astype(jnp.float32)
    label_pos = jnp.arange(LABELS, dtype=jnp.int32)[None, :]

    def block_step(carry, start):
        pred_acc, weight_acc, bias_acc = carry
        enc = lax.dynamic_slice_in_dim(encoder_out, start, FR_DEV, 0).astype(jnp.float32)
        alpha = lax.dynamic_slice_in_dim(alpha_saved, start, FR_DEV, 0)
        beta_b = lax.dynamic_slice_in_dim(beta_frame, start, FR_DEV, 0)
        beta_l = lax.dynamic_slice_in_dim(beta_label, start, FR_DEV, 0)
        joint = jnp.tanh(enc[:, None, :] + pred_f[None, :, :]).astype(jnp.bfloat16).reshape(FR_DEV * LABELS, H)
        logits = jnp.dot(joint, out_weight, preferred_element_type=jnp.float32) + out_bias[None, :]
        lse = jnp.log(jnp.sum(jnp.exp(logits), axis=-1))
        probs = jnp.exp(logits - lse[:, None]).reshape(FR_DEV, LABELS, V)
        logits3 = logits.reshape(FR_DEV, LABELS, V)
        lse2 = lse.reshape(FR_DEV, LABELS)
        lp_blank = logits3[:, :, 0] - lse2
        lp_label = jnp.sum(logits3 * label_hot[None, :, :], axis=-1) - lse2
        frame_pos = start + jnp.arange(FR_DEV, dtype=jnp.int32)[:, None]
        inner = (frame_pos < frame_len - 1) & (label_pos <= label_len)
        final = (frame_pos == frame_len - 1) & (label_pos == label_len)
        blank_ok = inner | final
        blank_arg = alpha + lp_blank + jnp.where(inner, beta_b, 0.0) - log_total
        blank_occ = jnp.where(blank_ok, jnp.exp(jnp.where(blank_ok, blank_arg, 0.0)), 0.0)
        label_ok = (frame_pos < frame_len) & (label_pos < label_len)
        label_arg = alpha + lp_label + beta_l - log_total
        label_occ = jnp.where(label_ok, jnp.exp(jnp.where(label_ok, label_arg, 0.0)), 0.0)
        grad_logits = ((blank_occ + label_occ)[:, :, None] * probs
                       - blank_occ[:, :, None] * blank_hot[None, None, :]
                       - label_occ[:, :, None] * label_hot[None, :, :]).astype(jnp.bfloat16).reshape(FR_DEV * LABELS, V)
        grad_joint = lax.dot_general(grad_logits, out_weight, (((1,), (1,)), ((), ())), preferred_element_type=jnp.float32)
        joint_f = joint.astype(jnp.float32)
        grad_pre = (grad_joint * (1.0 - joint_f * joint_f)).reshape(FR_DEV, LABELS, H)
        enc_grad = jnp.sum(grad_pre, axis=1)
        pred_acc = pred_acc + jnp.sum(grad_pre, axis=0)
        weight_acc = weight_acc + lax.dot_general(joint, grad_logits, (((0,), (0,)), ((), ())), preferred_element_type=jnp.float32)
        bias_acc = bias_acc + jnp.sum(grad_logits.astype(jnp.float32), axis=0)
        return (pred_acc, weight_acc, bias_acc), enc_grad

    starts = jnp.arange(FRAMES // FR_DEV, dtype=jnp.int32) * FR_DEV
    init = (jnp.zeros((LABELS, H), jnp.float32), jnp.zeros((H, V), jnp.float32), jnp.zeros((V,), jnp.float32))
    (grad_predictor, grad_weight, grad_bias), enc_blocks = lax.scan(block_step, init, starts)
    grad_encoder = enc_blocks.reshape(FRAMES, H)
    return grad_encoder, grad_predictor, grad_weight, grad_bias
```

```python
import functools

import jax
import jax.numpy as jnp
from jax import lax
from jax.experimental import pallas as pl
from jax.experimental.pallas import tpu as pltpu
from jax.sharding import PartitionSpec as P

MESH = pl.DeviceIdType.MESH
FR, LB, H, V = 96, 16, 640, 1024
GU = 4
ROWS = FR * GU
NX, NY, NZ = 4, 8, 8
HALF = 2560
A1, B, A2, C = 0, 768, 1280, 2048
F32, BF16 = jnp.float32, jnp.bfloat16


def place(x, y, z, c):
    return (x * 8 + (y % 4) * 2 + c, z * 2 + y // 4)


def rows(ref, start, size):
    return ref.at[pl.ds(pl.multiple_of(start, 8), size)]


def kernel(
    enc_ref, pred_ref, w_ref, bias_ref, labels_ref, lengths_ref, alpha_ref, beta_ref, ll_ref,
    out_ref, bias_out, enc_out, pred_out,
    encf, predf, joint, expo, grad, bsend, brow, bcol, asave, ssum, slab, sblank, occb, occl,
    bias_acc, peer_half, core_recv, acc, send_b,
    r1a1, r1b, r1a2, r1c, s1a1, s1a2, s1c, s2b, r2a1, r2b, r2a2, r2c,
    r3a1, r3b, r3a2, r3c,
    enc_acc, enc_t, e1_recv, e1_sum, e2_recv, tsq, pred_acc, pbuf, p1_recv, p2_recv, p3_recv,
    ssem, rsem,
):
    f = lax.axis_index("frames")
    l = lax.axis_index("labels")
    x, ylo, c = f // 8, (f // 2) % 4, f % 2
    z, yhi = l // 2, l % 2
    y = yhi * 4 + ylo
    other = 1 - c
    sibling = place(x, y, z, other)

    def xp(r):
        return place((x + r) % NX, y, z, c)

    def yp(r):
        return place(x, (y + r) % NY, z, c)

    def zp(r):
        return place(x, y, (z + r) % NZ, c)

    def send(src, dst, s, to):
        pltpu.make_async_remote_copy(
            src_ref=src, dst_ref=dst, send_sem=ssem.at[s], recv_sem=rsem.at[s],
            device_id=to, device_id_type=MESH,
        ).start()

    def arrived(s, ref):
        pltpu.make_async_copy(ref, ref, rsem.at[s]).wait()

    def left(s, ref):
        pltpu.make_async_copy(ref, ref, ssem.at[s]).wait()

    barrier = pltpu.get_barrier_semaphore()
    peers = [sibling]
    peers += [xp(r) for r in range(1, NX)] + [yp(r) for r in range(1, NY)] + [zp(r) for r in range(1, NZ)]
    peers += [((f + 1) % 32, l), (f, (l + 1) % 16)]
    for p in peers:
        pl.semaphore_signal(barrier, inc=1, device_id=p, device_id_type=MESH)

    encf[...] = enc_ref[...].astype(F32)
    predf[...] = pred_ref[...].astype(F32)
    bsend[...] = jnp.zeros_like(bsend)
    bsend[:, 0:LB] = beta_ref[...]
    asave[...] = jnp.zeros_like(asave)
    asave[:, 0:LB] = alpha_ref[...]
    ssum[...] = jnp.ones_like(ssum)
    slab[...] = jnp.zeros_like(slab)
    sblank[...] = jnp.zeros_like(sblank)
    lane = lax.broadcasted_iota(jnp.int32, (1, 128), 1)
    vocab = lax.broadcasted_iota(jnp.int32, (1, V), 1)

    def forward(g, _):
        for k in range(GU):
            u = g * GU + k
            start = pl.multiple_of(u * FR, 32)
            joint[pl.ds(start, FR)] = jnp.tanh(encf[...] + predf[pl.ds(u, 1)]).astype(BF16)
        first = pl.multiple_of(g * ROWS, 128)
        logits = jnp.dot(joint[pl.ds(first, ROWS)], w_ref[...], preferred_element_type=F32) + bias_ref[...]
        for k in range(GU):
            u = g * GU + k
            start = pl.multiple_of(u * FR, 32)
            part = logits[k * FR:(k + 1) * FR]
            e = jnp.exp(part)
            expo[pl.ds(start, FR)] = e
            hot = vocab == labels_ref[u]
            here = lane == u
            ssum[...] = jnp.where(here, jnp.sum(e, axis=1, keepdims=True), ssum[...])
            slab[...] = jnp.where(here, jnp.sum(jnp.where(hot, part, 0.0), axis=1, keepdims=True), slab[...])
            sblank[...] = jnp.where(here, part[:, 0:1], sblank[...])
        return 0

    forward(0, 0)
    pl.semaphore_wait(barrier, len(peers))
    send(bsend.at[pl.ds(0, 8)], brow, 0, ((f + 31) % 32, l))
    send(bsend, bcol, 1, (f, (l + 15) % 16))
    lax.fori_loop(1, LB // GU, forward, 0)

    arrived(0, brow)
    arrived(1, bcol)
    frame_len, label_len, log_total = lengths_ref[0], lengths_ref[1], ll_ref[0]
    t_here = lax.broadcasted_iota(jnp.int32, (FR, 128), 0)
    u_here = lax.broadcasted_iota(jnp.int32, (FR, 128), 1)
    t_pos, u_pos = t_here + f * FR, u_here + l * LB
    beta = bsend[...]
    beta_frame = jnp.where(t_here == FR - 1, brow[0:1, :], pltpu.roll(beta, FR - 1, 0))
    beta_label = jnp.where(u_here == LB - 1, bcol[:, 0:1], pltpu.roll(beta, 127, 1))
    total = ssum[...]
    lse = jnp.log(total)
    inner = (t_pos < frame_len - 1) & (u_pos <= label_len)
    final = (t_pos == frame_len - 1) & (u_pos == label_len)
    blank_ok = (inner | final) & (u_here < LB)
    blank_arg = asave[...] + (sblank[...] - lse) + jnp.where(inner, beta_frame, 0.0) - log_total
    occb[...] = jnp.where(blank_ok, jnp.exp(jnp.where(blank_ok, blank_arg, 0.0)), 0.0)
    label_ok = (t_pos < frame_len) & (u_pos < label_len) & (u_here < LB)
    label_arg = asave[...] + (slab[...] - lse) + beta_label - log_total
    occl[...] = jnp.where(label_ok, jnp.exp(jnp.where(label_ok, label_arg, 0.0)), 0.0)
    ssum[...] = 4.0 / total

    bias_acc[...] = jnp.zeros_like(bias_acc)

    def backward(u, _):
        here = lane == u
        start = pl.multiple_of(u * FR, 32)

        def column(ref):
            return jnp.sum(jnp.where(here, ref[...], 0.0), axis=1, keepdims=True)

        blank, label, inverse = column(occb), column(occl), column(ssum)
        quarter = (blank + label) * 0.25
        hot = vocab == labels_ref[u]
        g = (expo[pl.ds(start, FR)] * inverse) * quarter
        g = jnp.where(hot, g - label, g)
        g0 = jnp.where(lane == 0, g[:, 0:128] - blank, g[:, 0:128])
        grad[pl.ds(start, FR)] = g.astype(BF16)
        grad[pl.ds(start, FR), 0:128] = g0.astype(BF16)
        bias_acc[:, 128:] += jnp.sum(g[:, 128:].reshape(FR // 8, 8, V - 128), axis=0)
        bias_acc[:, 0:128] += jnp.sum(g0.reshape(FR // 8, 8, 128), axis=0)
        return 0

    lax.fori_loop(0, LB, backward, 0)

    def product(half, q, ref):
        base = pl.multiple_of(half * 512 + q * 256, 256)
        r = lax.dot_general(
            joint[...], grad[:, pl.ds(base, 256)], (((0,), (0,)), ((), ())), preferred_element_type=F32
        )
        ref[q * 1280:q * 1280 + 640] = r[:, 0:128]
        ref[q * 1280 + 640:q * 1280 + 1280] = r[:, 128:256]

    for q in range(2):
        product(other, q, peer_half)
        if q == 0:
            for k in range(8):
                peer_half[HALF + k:HALF + k + 1] = jnp.sum(bias_acc[:, k * 128:(k + 1) * 128], axis=0, keepdims=True)
            acc[HALF:HALF + 8] = peer_half[HALF:HALF + 8]
            send(rows(peer_half, HALF, 8), rows(core_recv, HALF, 8), 2, sibling)
        send(rows(peer_half, q * 1280, 1280), rows(core_recv, q * 1280, 1280), 3 + q, sibling)
    product(c, 0, acc)

    arrived(2, rows(core_recv, HALF, 8))
    arrived(3, rows(core_recv, 0, 1280))
    acc[0:768] += core_recv[0:768]
    for r in (2, 1, 3):
        send(rows(acc, A1 + (x + r) % NX * 192, 192), r1a1.at[r - 1], 5, xp(r))
    bias_tile = acc[HALF:HALF + 8] + core_recv[HALF:HALF + 8]
    for k in range(NY):
        send_b[k, 0:64] = acc[B + k * 64:B + k * 64 + 64] + core_recv[B + k * 64:B + k * 64 + 64]
        send_b[k, 64:72] = bias_tile
    for r in (4, 3, 5, 2, 6, 1, 7):
        send(send_b.at[(y + r) % NY], r1b.at[y], 6, yp(r))
    product(c, 1, acc)
    arrived(4, rows(core_recv, 1280, 1280))
    acc[1280:2560] += core_recv[1280:2560]
    for r in (2, 1, 3):
        send(rows(acc, A2 + (x + r) % NX * 192, 192), r1a2.at[r - 1], 7, xp(r))
    for r in (4, 3, 5, 2, 6, 1, 7):
        send(rows(acc, C + (z + r) % NZ * 64, 64), r1c.at[r - 1], 8, zp(r))
    r1b[y] = send_b[y]

    enc_acc[...] = jnp.zeros_like(enc_acc)

    def pre(g, _):
        first = pl.multiple_of(g * ROWS, 128)
        gj = lax.dot_general(
            grad[pl.ds(first, ROWS)], w_ref[...], (((1,), (1,)), ((), ())), preferred_element_type=F32
        )
        j = joint[pl.ds(first, ROWS)].astype(F32)
        gp = gj * (1.0 - j * j)
        enc_acc[0:FR] += (gp[0:FR] + gp[FR:2 * FR]) + (gp[2 * FR:3 * FR] + gp[3 * FR:4 * FR])
        for k in range(GU):
            pred_acc[pl.ds(g * GU + k, 1), 0:H] = jnp.sum(gp[k * FR:(k + 1) * FR], axis=0, keepdims=True)
        return 0

    pred_acc[...] = jnp.zeros_like(pred_acc)
    lax.fori_loop(0, LB // GU, pre, 0)
    for k in range(5):
        enc_t[k * 128:(k + 1) * 128] = jnp.transpose(enc_acc[:, k * 128:(k + 1) * 128])
    wide = pred_acc[...]
    for cc in range(2):
        for xx in range(4):
            for yy in range(4):
                start = (xx * 8 + yy * 2 + cc) * 20
                lo = start // 128 * 128
                two = wide[:, lo:lo + 256]
                pbuf[cc, xx, yy] = pltpu.roll(two, (256 - (start - lo)) % 256, 1)[:, 0:128]
    send(pbuf.at[other], p1_recv, 9, sibling)

    arrived(5, r1a1)
    s1a1[...] = (rows(acc, A1 + x * 192, 192)[...] + r1a1[0]) + (r1a1[1] + r1a1[2])
    for r in (4, 3, 5, 2, 6, 1, 7):
        send(rows(s1a1, (y + r) % NY * 24, 24), r2a1.at[r - 1], 10, yp(r))
    arrived(6, r1b.at[pl.ds(0, 7)])
    sum_b = r1b[0]
    for k in range(1, NY):
        sum_b = sum_b + r1b[k]
    for k in range(NZ):
        s2b[k, 0:8] = sum_b[k * 8:k * 8 + 8]
        s2b[k, 8:16] = sum_b[64:72]
    for r in (4, 3, 5, 2, 6, 1, 7):
        send(s2b.at[(z + r) % NZ], r2b.at[z], 11, zp(r))
    arrived(7, r1a2)
    s1a2[...] = (rows(acc, A2 + x * 192, 192)[...] + r1a2[0]) + (r1a2[1] + r1a2[2])
    for r in (4, 3, 5, 2, 6, 1, 7):
        send(rows(s1a2, (z + r) % NZ * 24, 24), r2a2.at[r - 1], 12, zp(r))
    arrived(8, r1c)
    sum_c = rows(acc, C + z * 64, 64)[...]
    for k in range(7):
        sum_c = sum_c + r1c[k]
    s1c[...] = sum_c
    for r in (4, 3, 5, 2, 6, 1, 7):
        send(rows(s1c, (y + r) % NY * 8, 8), r2c.at[r - 1], 13, yp(r))
    r2b[z] = s2b[z]

    for r in (4, 3, 5, 2, 6, 1, 7):
        send(rows(enc_t, (z + r) % NZ * 80, 80), e1_recv.at[r - 1], 14, zp(r))
    arrived(9, p1_recv)
    pbuf[c] = pbuf[c] + p1_recv[...]
    for r in (2, 1, 3):
        send(pbuf.at[c, (x + r) % NX], p2_recv.at[r - 1], 15, xp(r))

    arrived(10, r2a1)
    sum_a = rows(s1a1, y * 24, 24)[...]
    for k in range(7):
        sum_a = sum_a + r2a1[k]
    r3a1[z] = sum_a
    for r in (4, 3, 5, 2, 6, 1, 7):
        send(r3a1.at[z], r3a1.at[z], 16, zp(r))
    arrived(12, r2a2)
    sum_a = rows(s1a2, z * 24, 24)[...]
    for k in range(7):
        sum_a = sum_a + r2a2[k]
    r3a2[y] = sum_a
    for r in (4, 3, 5, 2, 6, 1, 7):
        send(r3a2.at[y], r3a2.at[y], 17, yp(r))
    arrived(11, r2b.at[pl.ds(0, 7)])
    sum_b = r2b[0]
    for k in range(1, NZ):
        sum_b = sum_b + r2b[k]
    r3b[x] = sum_b
    for r in (2, 1, 3):
        send(r3b.at[x], r3b.at[x], 18, xp(r))
    arrived(13, r2c)
    sum_c = rows(s1c, y * 8, 8)[...]
    for k in range(7):
        sum_c = sum_c + r2c[k]
    r3c[x] = sum_c
    for r in (2, 1, 3):
        send(r3c.at[x], r3c.at[x], 19, xp(r))

    base = c * HALF

    def spread(start, size, s, peer, order):
        piece = rows(out_ref, base + start, size)
        for r in order:
            send(piece, piece, s, peer(r))

    far8, far4 = (4, 3, 5, 2, 6, 1, 7), (2, 1, 3)
    arrived(16, r3a1.at[pl.ds(0, 7)])
    sum_a = r3a1[0]
    for k in range(1, NZ):
        sum_a = sum_a + r3a1[k]
    rows(out_ref, base + A1 + (x * 8 + y) * 24, 24)[...] = sum_a
    spread(A1 + (x * 8 + y) * 24, 24, 20, yp, far8)
    arrived(17, r3a2.at[pl.ds(0, 7)])
    sum_a = r3a2[0]
    for k in range(1, NY):
        sum_a = sum_a + r3a2[k]
    rows(out_ref, base + A2 + (x * 8 + z) * 24, 24)[...] = sum_a
    spread(A2 + (x * 8 + z) * 24, 24, 21, zp, far8)
    arrived(18, r3b.at[pl.ds(0, 3)])
    sum_b = (r3b[0] + r3b[1]) + (r3b[2] + r3b[3])
    rows(out_ref, base + B + (y * 8 + z) * 8, 8)[...] = sum_b[0:8]
    bias_out[...] = sum_b[8:16]
    spread(B + (y * 8 + z) * 8, 8, 22, zp, far8)
    arrived(19, r3c.at[pl.ds(0, 3)])
    rows(out_ref, base + C + (z * 8 + y) * 8, 8)[...] = (r3c[0] + r3c[1]) + (r3c[2] + r3c[3])
    spread(C + (z * 8 + y) * 8, 8, 23, yp, far8)

    arrived(14, e1_recv)
    e = rows(enc_t, z * 80, 80)[...]
    for k in range(7):
        e = e + e1_recv[k]
    e1_sum[...] = e
    send(rows(e1_sum, (1 - yhi) * 40, 40), e2_recv, 24, yp(4))
    arrived(15, p2_recv)
    pbuf[c, x] = (pbuf[c, x] + p2_recv[0]) + (p2_recv[1] + p2_recv[2])
    for r in (2, 1, 3):
        to = (ylo + r) % 4
        send(pbuf.at[c, x, to], p3_recv.at[r - 1], 25, place(x, yhi * 4 + to, z, c))

    arrived(20, rows(out_ref, 0, 168))
    spread(A1 + x * 192, 192, 26, xp, far4)
    arrived(21, rows(out_ref, 0, 168))
    spread(A2 + x * 192, 192, 27, xp, far4)
    arrived(22, rows(out_ref, 0, 56))
    spread(B + y * 64, 64, 28, yp, far8)
    arrived(23, rows(out_ref, 0, 56))
    spread(C + z * 64, 64, 29, zp, far8)

    arrived(24, e2_recv)
    tsq[...] = jnp.zeros_like(tsq)
    tsq[0:40] = rows(e1_sum, yhi * 40, 40)[...] + e2_recv[...]
    enc_out[...] = jnp.transpose(tsq[...])[0:FR, 0:40]
    arrived(25, p3_recv)
    pred_out[...] = ((pbuf[c, x, ylo] + p3_recv[0]) + (p3_recv[1] + p3_recv[2]))[:, 0:20]

    arrived(26, rows(out_ref, 0, 576))
    send(rows(out_ref, base + A1, 768), rows(out_ref, base + A1, 768), 30, sibling)
    arrived(27, rows(out_ref, 0, 576))
    send(rows(out_ref, base + A2, 768), rows(out_ref, base + A2, 768), 31, sibling)
    arrived(28, rows(out_ref, 0, 448))
    send(rows(out_ref, base + B, 512), rows(out_ref, base + B, 512), 32, sibling)
    arrived(29, rows(out_ref, 0, 448))
    send(rows(out_ref, base + C, 512), rows(out_ref, base + C, 512), 33, sibling)
    for s, n in ((30, 768), (31, 768), (32, 512), (33, 512)):
        arrived(s, rows(out_ref, 0, n))

    left(0, brow)
    left(1, bcol)
    for s, n in (
        (2, 8), (3, 1280), (4, 1280), (5, 576), (6, 504), (7, 576), (8, 448), (10, 168), (11, 112), (12, 168),
        (13, 56), (14, 560), (16, 168), (17, 168), (18, 48), (19, 24), (20, 168), (21, 168), (22, 56), (23, 56),
        (24, 40), (26, 576), (27, 576), (28, 448), (29, 448), (30, 768), (31, 768), (32, 512), (33, 512),
    ):
        left(s, rows(out_ref, 0, n))
    left(9, p1_recv)
    left(15, p2_recv)
    left(25, p3_recv)


def vm(*shape, dtype=F32):
    return pltpu.VMEM(shape, dtype)


def local(encoder_out, predictor_out, out_weight, out_bias, target_labels, lengths, alpha, beta, log_likelihood):
    vmem = pl.BlockSpec(memory_space=pltpu.VMEM)
    smem = pl.BlockSpec(memory_space=pltpu.SMEM)
    weight, bias, enc, pred = pl.pallas_call(
        kernel,
        out_shape=(
            jax.ShapeDtypeStruct((2 * HALF, 128), F32),
            jax.ShapeDtypeStruct((8, 128), F32),
            jax.ShapeDtypeStruct((FR, 40), F32),
            jax.ShapeDtypeStruct((LB, 20), F32),
        ),
        in_specs=[vmem, vmem, vmem, vmem, smem, smem, vmem, vmem, smem],
        out_specs=(vmem, vmem, vmem, vmem),
        scratch_shapes=[
            vm(FR, H), vm(LB, H), vm(FR * LB, H, dtype=BF16), vm(FR * LB, V), vm(FR * LB, V, dtype=BF16),
            vm(FR, 128), vm(8, 128), vm(FR, 128), vm(FR, 128), vm(FR, 128), vm(FR, 128), vm(FR, 128),
            vm(FR, 128), vm(FR, 128),
            vm(8, V), vm(HALF + 8, 128), vm(HALF + 8, 128), vm(HALF + 8, 128), vm(8, 72, 128),
            vm(3, 192, 128), vm(8, 72, 128), vm(3, 192, 128), vm(7, 64, 128),
            vm(192, 128), vm(192, 128), vm(64, 128), vm(8, 16, 128),
            vm(7, 24, 128), vm(8, 16, 128), vm(7, 24, 128), vm(7, 8, 128),
            vm(8, 24, 128), vm(4, 16, 128), vm(8, 24, 128), vm(4, 8, 128),
            vm(128, H), vm(H, 128), vm(7, 80, 128), vm(80, 128), vm(40, 128), vm(128, 128),
            vm(LB, 768), vm(2, 4, 4, LB, 128), vm(4, 4, LB, 128), vm(3, 4, LB, 128), vm(3, LB, 128),
            pltpu.SemaphoreType.DMA((34,)), pltpu.SemaphoreType.DMA((34,)),
        ],
        compiler_params=pltpu.CompilerParams(
            collective_id=0, has_side_effects=True, vmem_limit_bytes=56 * 2**20
        ),
        name="joint_backward",
    )(
        encoder_out, predictor_out, out_weight, out_bias.reshape(1, V), target_labels, lengths, alpha, beta,
        log_likelihood,
    )
    grad_weight = weight.reshape(8, H, 128).transpose(1, 0, 2).reshape(H, V)
    return enc, pred, grad_weight, bias.reshape(V)


def solution(mesh):
    placed = (
        P("frames", None), P("labels", None), P(), P(), P("labels"), P(),
        P("frames", "labels"), P("frames", "labels"), P(),
    )
    return jax.shard_map(
        local,
        mesh=mesh,
        in_specs=placed,
        out_specs=(P("frames", "labels"), P("labels", "frames"), P(), P()),
        check_vma=False,
    )
```

```python
import jax
import jax.numpy as jnp
from jax import lax
from jax.experimental import pallas as pl
from jax.experimental.pallas import tpu as pltpu
from jax.sharding import PartitionSpec as P

MESH = pl.DeviceIdType.MESH
FR, LB, H, V = 96, 16, 640, 1024
GU = 4
ROWS = FR * GU
NX, NY, NZ = 4, 8, 8
HALF = 2560
A1, B, A2, C = 0, 768, 1280, 2048
SEMS = 80
F32, BF16 = jnp.float32, jnp.bfloat16


def place(x, y, z, c):
    return (x * 8 + (y % 4) * 2 + c, z * 2 + y // 4)


def rows(ref, start, size):
    return ref.at[pl.ds(pl.multiple_of(start, 8), size)]


def kernel(
    enc_in, pred_in, w_in, bias_in, labels_in, lengths_in, alpha_in, beta_in, ll_ref,
    out_ref, bias_out, enc_out, pred_out,
    enc_ref, pred_ref, w_ref, bias_ref, labels_ref, lengths_ref, alpha_ref, beta_ref, isem,
    encf, predf, joint, expo, grad, bsend, brow, bcol, turn, ssum, slab, sblank, occb, occl,
    bias_acc, peer_half, core_recv, acc, send_b,
    r1a1, r1b, r1a2, r1c, s1a1, s1a2, s1c, s2b, r2a1, r2b, r2a2, r2c,
    r3a1, r3b, r3a2, r3c,
    enc_acc, enc_t, e_up, e_down, e_sum, e_last, pred_acc, pbuf, p1_recv, p2_recv, p3_recv,
    ssem, rsem,
):
    f = lax.axis_index("frames")
    l = lax.axis_index("labels")
    x, ylo, c = f // 8, (f // 2) % 4, f % 2
    z, yhi = l // 2, l % 2
    y = yhi * 4 + ylo
    other = 1 - c
    sibling = place(x, y, z, other)
    far8, near8, far4, near4 = (4, 3, 5, 2, 6, 1, 7), (1, 7, 2, 6, 3, 5, 4), (2, 1, 3), (1, 3, 2)

    def xp(r):
        return place((x + r) % NX, y, z, c)

    def yp(r):
        return place(x, (y + r) % NY, z, c)

    def zp(r):
        return place(x, y, (z + r) % NZ, c)

    index, amount = {}, {}

    def send(src, dst, kind, to):
        k = index.setdefault(kind, len(index))
        size = 1
        for n in src.shape[:-1]:
            size *= n
        amount[kind] = amount.get(kind, 0) + size
        pltpu.make_async_remote_copy(
            src_ref=src, dst_ref=dst, send_sem=ssem.at[k], recv_sem=rsem.at[k],
            device_id=to, device_id_type=MESH,
        ).start()

    def wait(sem, kind):
        ref = out_ref.at[pl.ds(0, amount[kind])]
        pltpu.make_async_copy(ref, ref, sem.at[index[kind]]).wait()

    def arrived(kind):
        wait(rsem, kind)

    loads = [
        pltpu.make_async_copy(src, dst, isem.at[k])
        for k, (src, dst) in enumerate((
            (enc_in, enc_ref), (pred_in, pred_ref), (beta_in, beta_ref), (alpha_in, alpha_ref), (bias_in, bias_ref),
            (labels_in, labels_ref), (lengths_in, lengths_ref), (w_in, w_ref),
        ))
    ]
    for load in loads:
        load.start()

    barrier = pltpu.get_barrier_semaphore()
    peers = [sibling]
    peers += [xp(r) for r in range(1, NX)] + [yp(r) for r in range(1, NY)] + [zp(r) for r in range(1, NZ)]
    peers += [((f + 1) % 32, l), (f, (l + 1) % 16)]
    for p in peers:
        pl.semaphore_signal(barrier, inc=1, device_id=p, device_id_type=MESH)

    for load in loads:
        load.wait()

    encf[...] = enc_ref[...].astype(F32)
    predf[...] = pred_ref[...].astype(F32)
    bsend[...] = jnp.zeros_like(bsend)
    bsend[:, 0:FR] = beta_ref[...]
    turn[...] = jnp.zeros_like(turn)
    turn[0, 0:LB, 0:FR] = alpha_ref[...]
    ssum[...] = jnp.ones_like(ssum)
    slab[...] = jnp.zeros_like(slab)
    sblank[...] = jnp.zeros_like(sblank)
    lane = lax.broadcasted_iota(jnp.int32, (1, 128), 1)
    vocab = lax.broadcasted_iota(jnp.int32, (1, V), 1)

    def forward(g, _):
        for k in range(GU):
            u = g * GU + k
            start = pl.multiple_of(u * FR, 32)
            joint[pl.ds(start, FR)] = jnp.tanh(encf[...] + predf[pl.ds(u, 1)]).astype(BF16)
        first = pl.multiple_of(g * ROWS, 128)
        logits = jnp.dot(joint[pl.ds(first, ROWS)], w_ref[...], preferred_element_type=F32) + bias_ref[...]
        for k in range(GU):
            u = g * GU + k
            start = pl.multiple_of(u * FR, 32)
            part = logits[k * FR:(k + 1) * FR]
            e = jnp.exp(part)
            expo[pl.ds(start, FR)] = e
            hot = vocab == labels_ref[u]
            here = lane == u
            ssum[...] = jnp.where(here, jnp.sum(e, axis=1, keepdims=True), ssum[...])
            slab[...] = jnp.where(here, jnp.sum(jnp.where(hot, part, 0.0), axis=1, keepdims=True), slab[...])
            sblank[...] = jnp.where(here, part[:, 0:1], sblank[...])
        return 0

    forward(0, 0)
    pl.semaphore_wait(barrier, len(peers))
    send(bsend, brow, "frame", ((f + 31) % 32, l))
    send(bsend.at[pl.ds(0, 8)], bcol, "label", (f, (l + 15) % 16))
    lax.fori_loop(1, LB // GU, forward, 0)

    arrived("frame")
    arrived("label")
    frame_len, label_len, log_total = lengths_ref[0], lengths_ref[1], ll_ref[0]
    beta = bsend[...]
    label_row = lax.broadcasted_iota(jnp.int32, (LB, 128), 0)
    turn[1, 0:LB] = jnp.where(lane == FR - 1, brow[:, 0:1], pltpu.roll(beta, 127, 1))
    turn[2, 0:LB] = jnp.where(label_row == LB - 1, bcol[0:1, :], pltpu.roll(beta, LB - 1, 0))
    alpha = jnp.transpose(turn[0])[0:FR]
    beta_frame = jnp.transpose(turn[1])[0:FR]
    beta_label = jnp.transpose(turn[2])[0:FR]
    t_pos = lax.broadcasted_iota(jnp.int32, (FR, 128), 0) + f * FR
    u_here = lax.broadcasted_iota(jnp.int32, (FR, 128), 1)
    u_pos = u_here + l * LB
    total = ssum[...]
    lse = jnp.log(total)
    inner = (t_pos < frame_len - 1) & (u_pos <= label_len)
    final = (t_pos == frame_len - 1) & (u_pos == label_len)
    blank_ok = (inner | final) & (u_here < LB)
    blank_arg = alpha + (sblank[...] - lse) + jnp.where(inner, beta_frame, 0.0) - log_total
    occb[...] = jnp.where(blank_ok, jnp.exp(jnp.where(blank_ok, blank_arg, 0.0)), 0.0)
    label_ok = (t_pos < frame_len) & (u_pos < label_len) & (u_here < LB)
    label_arg = alpha + (slab[...] - lse) + beta_label - log_total
    occl[...] = jnp.where(label_ok, jnp.exp(jnp.where(label_ok, label_arg, 0.0)), 0.0)
    ssum[...] = 4.0 / total

    bias_acc[...] = jnp.zeros_like(bias_acc)

    def backward(u, _):
        here = lane == u
        start = pl.multiple_of(u * FR, 32)

        def column(ref):
            return jnp.sum(jnp.where(here, ref[...], 0.0), axis=1, keepdims=True)

        blank, label, inverse = column(occb), column(occl), column(ssum)
        quarter = (blank + label) * 0.25
        hot = vocab == labels_ref[u]
        g = (expo[pl.ds(start, FR)] * inverse) * quarter
        g = jnp.where(hot, g - label, g)
        g0 = jnp.where(lane == 0, g[:, 0:128] - blank, g[:, 0:128])
        grad[pl.ds(start, FR)] = g.astype(BF16)
        grad[pl.ds(start, FR), 0:128] = g0.astype(BF16)
        bias_acc[:, 128:] += jnp.sum(g[:, 128:].reshape(FR // 8, 8, V - 128), axis=0)
        bias_acc[:, 0:128] += jnp.sum(g0.reshape(FR // 8, 8, 128), axis=0)
        return 0

    lax.fori_loop(0, LB, backward, 0)

    def product(half, q, ref):
        base = pl.multiple_of(half * 512 + q * 256, 256)
        r = lax.dot_general(
            joint[...], grad[:, pl.ds(base, 256)], (((0,), (0,)), ((), ())), preferred_element_type=F32
        )
        ref[q * 1280:q * 1280 + 640] = r[:, 0:128]
        ref[q * 1280 + 640:q * 1280 + 1280] = r[:, 128:256]

    for q in range(2):
        product(other, q, peer_half)
        if q == 0:
            for k in range(8):
                peer_half[HALF + k:HALF + k + 1] = jnp.sum(bias_acc[:, k * 128:(k + 1) * 128], axis=0, keepdims=True)
            acc[HALF:HALF + 8] = peer_half[HALF:HALF + 8]
            send(rows(peer_half, HALF, 8), rows(core_recv, HALF, 8), "bias", sibling)
        send(rows(peer_half, q * 1280, 1280), rows(core_recv, q * 1280, 1280), ("half", q), sibling)
    product(c, 0, acc)

    arrived("bias")
    arrived(("half", 0))
    acc[0:768] += core_recv[0:768]
    for r in far4:
        send(rows(acc, A1 + (x + r) % NX * 192, 192), r1a1.at[r - 1], "a1 1", xp(r))
    bias_tile = acc[HALF:HALF + 8] + core_recv[HALF:HALF + 8]
    for k in range(NY):
        send_b[k, 0:64] = acc[B + k * 64:B + k * 64 + 64] + core_recv[B + k * 64:B + k * 64 + 64]
        send_b[k, 64:72] = bias_tile
    for r in far8:
        send(send_b.at[(y + r) % NY], r1b.at[y], "b 1", yp(r))
    product(c, 1, acc)
    arrived(("half", 1))
    acc[1280:2560] += core_recv[1280:2560]
    for r in far4:
        send(rows(acc, A2 + (x + r) % NX * 192, 192), r1a2.at[r - 1], "a2 1", xp(r))
    for r in far8:
        send(rows(acc, C + (z + r) % NZ * 64, 64), r1c.at[r - 1], "c 1", zp(r))
    r1b[y] = send_b[y]

    enc_acc[...] = jnp.zeros_like(enc_acc)

    def pre(g, _):
        first = pl.multiple_of(g * ROWS, 128)
        gj = lax.dot_general(
            grad[pl.ds(first, ROWS)], w_ref[...], (((1,), (1,)), ((), ())), preferred_element_type=F32
        )
        j = joint[pl.ds(first, ROWS)].astype(F32)
        gp = gj * (1.0 - j * j)
        enc_acc[0:FR] += (gp[0:FR] + gp[FR:2 * FR]) + (gp[2 * FR:3 * FR] + gp[3 * FR:4 * FR])
        for k in range(GU):
            pred_acc[pl.ds(g * GU + k, 1), 0:H] = jnp.sum(gp[k * FR:(k + 1) * FR], axis=0, keepdims=True)
        return 0

    pred_acc[...] = jnp.zeros_like(pred_acc)
    lax.fori_loop(0, LB // GU, pre, 0)
    for k in range(5):
        enc_t[k * 128:(k + 1) * 128] = jnp.transpose(enc_acc[:, k * 128:(k + 1) * 128])

    def piece(r):
        return rows(enc_t, (z + r) % NZ * 80, 80)

    send(piece(4), e_up.at[0], "e up 0", zp(1))
    wide = pred_acc[...]
    for cc in range(2):
        for xx in range(4):
            for yy in range(4):
                start = (xx * 8 + yy * 2 + cc) * 20
                lo = start // 128 * 128
                two = wide[:, lo:lo + 256]
                pbuf[cc, xx, yy] = pltpu.roll(two, (256 - (start - lo)) % 256, 1)[:, 0:128]
    send(pbuf.at[other], p1_recv, "p 1", sibling)

    arrived("a1 1")
    s1a1[...] = (rows(acc, A1 + x * 192, 192)[...] + r1a1[0]) + (r1a1[1] + r1a1[2])
    for r in far8:
        send(rows(s1a1, (y + r) % NY * 24, 24), r2a1.at[r - 1], "a1 2", yp(r))
    arrived("b 1")
    sum_b = r1b[0]
    for k in range(1, NY):
        sum_b = sum_b + r1b[k]
    for k in range(NZ):
        s2b[k, 0:8] = sum_b[k * 8:k * 8 + 8]
        s2b[k, 8:16] = sum_b[64:72]
    for r in far8:
        send(s2b.at[(z + r) % NZ], r2b.at[z], "b 2", zp(r))
    arrived("a2 1")
    s1a2[...] = (rows(acc, A2 + x * 192, 192)[...] + r1a2[0]) + (r1a2[1] + r1a2[2])
    for r in far8:
        send(rows(s1a2, (z + r) % NZ * 24, 24), r2a2.at[r - 1], "a2 2", zp(r))
    arrived("c 1")
    sum_c = rows(acc, C + z * 64, 64)[...]
    for k in range(7):
        sum_c = sum_c + r1c[k]
    s1c[...] = sum_c
    for r in far8:
        send(rows(s1c, (y + r) % NY * 8, 8), r2c.at[r - 1], "c 2", yp(r))
    r2b[z] = s2b[z]

    arrived("e up 0")
    e_up[0] += piece(3)[...]
    send(e_up.at[0], e_up.at[1], "e up 1", zp(1))
    send(piece(5), e_down.at[0], "e down 0", zp(7))
    arrived("p 1")
    pbuf[c] = pbuf[c] + p1_recv[...]
    for r in far4:
        send(pbuf.at[c, (x + r) % NX], p2_recv.at[r - 1], "p 2", xp(r))

    arrived("b 2")
    sum_b = r2b[0]
    for k in range(1, NZ):
        sum_b = sum_b + r2b[k]
    r3b[x] = sum_b
    for r in far4:
        send(r3b.at[x], r3b.at[x], "b 3", xp(r))
    arrived("a1 2")
    sum_a = rows(s1a1, y * 24, 24)[...]
    for k in range(7):
        sum_a = sum_a + r2a1[k]
    r3a1[z] = sum_a
    for r in far8:
        send(r3a1.at[z], r3a1.at[z], "a1 3", zp(r))
    arrived("a2 2")
    sum_a = rows(s1a2, z * 24, 24)[...]
    for k in range(7):
        sum_a = sum_a + r2a2[k]
    r3a2[y] = sum_a
    for r in far8:
        send(r3a2.at[y], r3a2.at[y], "a2 3", yp(r))
    arrived("c 2")
    sum_c = rows(s1c, y * 8, 8)[...]
    for k in range(7):
        sum_c = sum_c + r2c[k]
    r3c[x] = sum_c
    for r in far4:
        send(r3c.at[x], r3c.at[x], "c 3", xp(r))

    arrived("e up 1")
    e_up[1] += piece(2)[...]
    send(e_up.at[1], e_up.at[2], "e up 2", zp(1))
    arrived("e down 0")
    e_down[0] += piece(6)[...]
    send(e_down.at[0], e_down.at[1], "e down 1", zp(7))
    arrived("p 2")
    pbuf[c, x] = (pbuf[c, x] + p2_recv[0]) + (p2_recv[1] + p2_recv[2])
    for r in far4:
        to = (ylo + r) % 4
        send(pbuf.at[c, x, to], p3_recv.at[r - 1], "p 3", place(x, yhi * 4 + to, z, c))

    base = c * HALF

    def spread(start, size, kind, peer, order, apart=False):
        part = rows(out_ref, base + start, size)
        for r in order:
            send(part, part, (kind, r) if apart else kind, peer(r))

    def across(start, size):
        part = rows(out_ref, base + start, size)
        send(part, part, "core", sibling)

    arrived("b 3")
    sum_b = (r3b[0] + r3b[1]) + (r3b[2] + r3b[3])
    rows(out_ref, base + B + (y * 8 + z) * 8, 8)[...] = sum_b[0:8]
    bias_out[...] = sum_b[8:16]
    spread(B + (y * 8 + z) * 8, 8, "b z", zp, far8)
    arrived("a1 3")
    sum_a = r3a1[0]
    for k in range(1, NZ):
        sum_a = sum_a + r3a1[k]
    rows(out_ref, base + A1 + (x * 8 + y) * 24, 24)[...] = sum_a
    spread(A1 + (x * 8 + y) * 24, 24, "a1 y", yp, far8, True)
    spread(A1 + (x * 8 + y) * 24, 24, "a1 x", xp, far4, True)
    arrived("a2 3")
    sum_a = r3a2[0]
    for k in range(1, NY):
        sum_a = sum_a + r3a2[k]
    rows(out_ref, base + A2 + (x * 8 + z) * 24, 24)[...] = sum_a
    spread(A2 + (x * 8 + z) * 24, 24, "a2 z", zp, far8, True)
    spread(A2 + (x * 8 + z) * 24, 24, "a2 x", xp, far4, True)
    arrived("c 3")
    rows(out_ref, base + C + (z * 8 + y) * 8, 8)[...] = (r3c[0] + r3c[1]) + (r3c[2] + r3c[3])
    spread(C + (z * 8 + y) * 8, 8, "c y", yp, far8)

    arrived("e up 2")
    e_up[2] += piece(1)[...]
    send(e_up.at[2], e_up.at[3], "e up 3", zp(1))
    arrived("e down 1")
    e_down[1] += piece(7)[...]
    send(e_down.at[1], e_down.at[2], "e down 2", zp(7))

    for n, r in enumerate(near8):
        arrived(("a1 y", r))
        spread(A1 + (x * 8 + (y + NY - r) % NY) * 24, 24, "a1 x", xp, far4, True)
        arrived(("a2 z", r))
        spread(A2 + (x * 8 + (z + NZ - r) % NZ) * 24, 24, "a2 x", xp, far4, True)
        if n == 3:
            arrived("b z")
            spread(B + y * 64, 64, "b y", yp, far8, True)
            arrived("c y")
            spread(C + z * 64, 64, "c z", zp, far8, True)
    across(A1 + x * 192, 192)
    across(A2 + x * 192, 192)
    across(B + y * 64, 64)
    across(C + z * 64, 64)

    arrived("e up 3")
    arrived("e down 2")
    e_sum[...] = piece(0)[...] + (e_up[3] + e_down[2])
    send(rows(e_sum, (1 - yhi) * 40, 40), e_last, "e y", yp(4))
    arrived("p 3")
    pred_out[...] = ((pbuf[c, x, ylo] + p3_recv[0]) + (p3_recv[1] + p3_recv[2]))[:, 0:20]

    for r in near8:
        arrived(("b y", r))
        across(B + (y + NY - r) % NY * 64, 64)
        arrived(("c z", r))
        across(C + (z + NZ - r) % NZ * 64, 64)
    for r in near4:
        arrived(("a1 x", r))
        across(A1 + (x + NX - r) % NX * 192, 192)
        arrived(("a2 x", r))
        across(A2 + (x + NX - r) % NX * 192, 192)
    arrived("e y")
    enc_out[...] = (rows(e_sum, yhi * 40, 40)[...] + e_last[...])[:, 0:FR]
    arrived("core")

    for kind in index:
        wait(ssem, kind)


def finish(weight, bias, enc, pred, weight_out, bias_out, enc_out, pred_out, sem):
    copies = [
        pltpu.make_async_copy(rows(weight, k * H, H), weight_out.at[:, pl.ds(k * 128, 128)], sem.at[k])
        for k in range(8)
    ]
    copies += [
        pltpu.make_async_copy(src, dst, sem.at[8 + k])
        for k, (src, dst) in enumerate(((bias, bias_out), (enc, enc_out), (pred, pred_out)))
    ]
    for copy in copies:
        copy.start()
    for copy in copies:
        copy.wait()


def vm(*shape, dtype=F32):
    return pltpu.VMEM(shape, dtype)


def local(encoder_out, predictor_out, out_weight, out_bias, target_labels, lengths, alpha, beta, log_likelihood):
    vmem = pl.BlockSpec(memory_space=pltpu.VMEM)
    hbm = pl.BlockSpec(memory_space=pltpu.HBM)
    sums = pl.pallas_call(
        kernel,
        out_shape=(vm(2 * HALF, 128), vm(8, 128), vm(40, FR), vm(LB, 20)),
        in_specs=[hbm] * 8 + [pl.BlockSpec(memory_space=pltpu.SMEM)],
        out_specs=(vmem, vmem, vmem, vmem),
        scratch_shapes=[
            vm(FR, H, dtype=BF16), vm(LB, H, dtype=BF16), vm(H, V, dtype=BF16), vm(1, V),
            pltpu.SMEM((LB,), jnp.int32), pltpu.SMEM((2,), jnp.int32), vm(LB, FR), vm(LB, FR),
            pltpu.SemaphoreType.DMA((8,)),
            vm(FR, H), vm(LB, H), vm(FR * LB, H, dtype=BF16), vm(FR * LB, V), vm(FR * LB, V, dtype=BF16),
            vm(LB, 128), vm(LB, 128), vm(8, 128), vm(3, 128, 128), vm(FR, 128), vm(FR, 128), vm(FR, 128),
            vm(FR, 128), vm(FR, 128),
            vm(8, V), vm(HALF + 8, 128), vm(HALF + 8, 128), vm(HALF + 8, 128), vm(8, 72, 128),
            vm(3, 192, 128), vm(8, 72, 128), vm(3, 192, 128), vm(7, 64, 128),
            vm(192, 128), vm(192, 128), vm(64, 128), vm(8, 16, 128),
            vm(7, 24, 128), vm(8, 16, 128), vm(7, 24, 128), vm(7, 8, 128),
            vm(8, 24, 128), vm(4, 16, 128), vm(8, 24, 128), vm(4, 8, 128),
            vm(128, H), vm(H, 128), vm(4, 80, 128), vm(3, 80, 128), vm(80, 128), vm(40, 128),
            vm(LB, 768), vm(2, 4, 4, LB, 128), vm(4, 4, LB, 128), vm(3, 4, LB, 128), vm(3, LB, 128),
            pltpu.SemaphoreType.DMA((SEMS,)), pltpu.SemaphoreType.DMA((SEMS,)),
        ],
        compiler_params=pltpu.CompilerParams(
            collective_id=0, has_side_effects=True, vmem_limit_bytes=44 * 2**20
        ),
        name="joint_backward",
    )(*(
        pltpu.with_memory_space_constraint(a, pltpu.HBM) for a in (
            encoder_out, predictor_out, out_weight, out_bias.reshape(1, V), target_labels, lengths, alpha.T, beta.T,
        )
    ), log_likelihood)
    weight, bias, enc, pred = pl.pallas_call(
        finish,
        out_shape=(
            jax.ShapeDtypeStruct((H, V), F32),
            jax.ShapeDtypeStruct((8, 128), F32),
            jax.ShapeDtypeStruct((40, FR), F32),
            jax.ShapeDtypeStruct((LB, 20), F32),
        ),
        in_specs=[pl.BlockSpec(memory_space=pl.ANY)] * 4,
        out_specs=[hbm] * 4,
        scratch_shapes=[pltpu.SemaphoreType.DMA((11,))],
        compiler_params=pltpu.CompilerParams(vmem_limit_bytes=2 * 2**20),
        name="finish",
    )(*sums)
    return enc.T, pred, weight, bias.reshape(V)


def solution(mesh):
    placed = (
        P("frames", None), P("labels", None), P(), P(), P("labels"), P(),
        P("frames", "labels"), P("frames", "labels"), P(),
    )
    return jax.shard_map(
        local,
        mesh=mesh,
        in_specs=placed,
        out_specs=(P("frames", "labels"), P("labels", "frames"), P(), P()),
        check_vma=False,
    )
```

```python
import jax
import jax.numpy as jnp
from jax import lax
from jax.experimental import pallas as pl
from jax.experimental.pallas import tpu as pltpu
from jax.sharding import PartitionSpec as P

MESH = pl.DeviceIdType.MESH
FR, LB, H, V = 96, 16, 640, 1024
GU = 4
ROWS = FR * GU
NX, NY, NZ = 4, 8, 8
HALF = 2560
A1, B, A2, C = 0, 768, 1280, 2048
SEMS = 80
F32, BF16 = jnp.float32, jnp.bfloat16


def place(x, y, z, c):
    return (x * 8 + (y % 4) * 2 + c, z * 2 + y // 4)


def rows(ref, start, size):
    return ref.at[pl.ds(pl.multiple_of(start, 8), size)]


def kernel(
    enc_in, pred_in, w_in, bias_in, labels_in, lengths_in, alpha_in, beta_in, ll_ref,
    out_ref, bias_out, enc_out, pred_out,
    enc_ref, pred_ref, w_ref, bias_ref, labels_ref, lengths_ref, alpha_ref, beta_ref, isem,
    encf, predf, joint, expo, grad, bsend, brow, bcol, turn, alpha_t, total, ssum, slab, sblank, occb, occl,
    bias_acc, peer_half, core_recv, acc, send_b,
    r1a1, r1b, r1a2, r1c, s1a1, s1a2, s1c, s2b, r2a1, r2b, r2a2, r2c,
    r3a1, r3b, r3a2, r3c,
    enc_acc, enc_t, e_up, e_down, e_sum, e_last, pred_acc, pbuf, p1_recv, p2_recv, p3_recv,
    ssem, rsem,
):
    f = lax.axis_index("frames")
    l = lax.axis_index("labels")
    x, ylo, c = f // 8, (f // 2) % 4, f % 2
    z, yhi = l // 2, l % 2
    y = yhi * 4 + ylo
    other = 1 - c
    sibling = place(x, y, z, other)
    far8, near8, far4, near4 = (4, 3, 5, 2, 6, 1, 7), (1, 7, 2, 6, 3, 5, 4), (2, 1, 3), (1, 3, 2)

    def xp(r):
        return place((x + r) % NX, y, z, c)

    def yp(r):
        return place(x, (y + r) % NY, z, c)

    def zp(r):
        return place(x, y, (z + r) % NZ, c)

    index, amount = {}, {}

    def send(src, dst, kind, to):
        k = index.setdefault(kind, len(index))
        size = 1
        for n in src.shape[:-1]:
            size *= n
        amount[kind] = amount.get(kind, 0) + size
        pltpu.make_async_remote_copy(
            src_ref=src, dst_ref=dst, send_sem=ssem.at[k], recv_sem=rsem.at[k],
            device_id=to, device_id_type=MESH,
        ).start()

    def wait(sem, kind):
        ref = out_ref.at[pl.ds(0, amount[kind])]
        pltpu.make_async_copy(ref, ref, sem.at[index[kind]]).wait()

    def arrived(kind):
        wait(rsem, kind)

    gone = set()

    def drain(kinds):
        for kind in kinds:
            if kind not in gone:
                gone.add(kind)
                wait(ssem, kind)

    loads = [
        pltpu.make_async_copy(src, dst, isem.at[k])
        for k, (src, dst) in enumerate((
            (enc_in, enc_ref), (pred_in, pred_ref), (w_in, w_ref), (beta_in, beta_ref), (alpha_in, alpha_ref),
            (bias_in, bias_ref), (labels_in, labels_ref), (lengths_in, lengths_ref),
        ))
    ]
    for load in loads:
        load.start()

    barrier = pltpu.get_barrier_semaphore()
    peers = [sibling]
    peers += [xp(r) for r in range(1, NX)] + [yp(r) for r in range(1, NY)] + [zp(r) for r in range(1, NZ)]
    peers += [((f + 1) % 32, l), (f, (l + 1) % 16)]
    for p in peers:
        pl.semaphore_signal(barrier, inc=1, device_id=p, device_id_type=MESH)

    lane = lax.broadcasted_iota(jnp.int32, (1, 128), 1)
    vocab = lax.broadcasted_iota(jnp.int32, (1, V), 1)

    def squash(g):
        for k in range(GU):
            u = g * GU + k
            joint[u * FR:(u + 1) * FR] = jnp.tanh(encf[...] + predf[u:u + 1]).astype(BF16)

    def forward(g):
        logits = jnp.dot(joint[g * ROWS:(g + 1) * ROWS], w_ref[...], preferred_element_type=F32) + bias_ref[...]
        for k in range(GU):
            u = g * GU + k
            part = logits[k * FR:(k + 1) * FR]
            e = jnp.exp(part)
            expo[u * FR:(u + 1) * FR] = e
            hot = vocab == labels_ref[u]
            here = lane == u
            ssum[...] = jnp.where(here, jnp.sum(e, axis=1, keepdims=True), ssum[...])
            slab[...] = jnp.where(here, jnp.sum(jnp.where(hot, part, 0.0), axis=1, keepdims=True), slab[...])
            sblank[...] = jnp.where(here, part[:, 0:1], sblank[...])

    loads[0].wait()
    loads[1].wait()
    encf[...] = enc_ref[...].astype(F32)
    predf[...] = pred_ref[...].astype(F32)
    ssum[...] = jnp.ones_like(ssum)
    slab[...] = jnp.zeros_like(slab)
    sblank[...] = jnp.zeros_like(sblank)
    squash(0)
    for load in loads[2:]:
        load.wait()
    bsend[...] = jnp.zeros_like(bsend)
    bsend[:, 0:FR] = beta_ref[...]
    turn[...] = jnp.zeros_like(turn)
    turn[0, 0:LB, 0:FR] = alpha_ref[...]
    squash(1)
    forward(0)
    pl.semaphore_wait(barrier, len(peers))
    send(bsend, brow, "frame", ((f + 31) % 32, l))
    send(bsend.at[pl.ds(0, 8)], bcol, "label", (f, (l + 15) % 16))
    squash(2)
    forward(1)
    squash(3)
    forward(2)
    forward(3)

    frame_len, label_len, log_total = lengths_ref[0], lengths_ref[1], ll_ref[0]
    label_row = lax.broadcasted_iota(jnp.int32, (LB, 128), 0)
    t_pos = lax.broadcasted_iota(jnp.int32, (FR, 128), 0) + f * FR
    u_here = lax.broadcasted_iota(jnp.int32, (FR, 128), 1)
    u_pos = u_here + l * LB
    total[...] = ssum[...]
    ssum[...] = 4.0 / total[...]
    alpha_t[...] = jnp.transpose(turn[0])[0:FR]

    def occupancies(next_frame, next_label):
        turn[1, 0:LB] = next_frame
        turn[2, 0:LB] = next_label
        alpha = alpha_t[...]
        beta_frame = jnp.transpose(turn[1])[0:FR]
        beta_label = jnp.transpose(turn[2])[0:FR]
        lse = jnp.log(total[...])
        inner = (t_pos < frame_len - 1) & (u_pos <= label_len)
        final = (t_pos == frame_len - 1) & (u_pos == label_len)
        blank_ok = (inner | final) & (u_here < LB)
        blank_arg = alpha + (sblank[...] - lse) + jnp.where(inner, beta_frame, 0.0) - log_total
        occb[...] = jnp.where(blank_ok, jnp.exp(jnp.where(blank_ok, blank_arg, 0.0)), 0.0)
        label_ok = (t_pos < frame_len) & (u_pos < label_len) & (u_here < LB)
        label_arg = alpha + (slab[...] - lse) + beta_label - log_total
        occl[...] = jnp.where(label_ok, jnp.exp(jnp.where(label_ok, label_arg, 0.0)), 0.0)

    bias_acc[...] = jnp.zeros_like(bias_acc)

    def backward(u, low, count):
        start = u * FR + low
        blank, label, inverse = (ref[low:low + count, u:u + 1] for ref in (occb, occl, ssum))
        quarter = (blank + label) * 0.25
        hot = vocab == labels_ref[u]
        g = (expo[start:start + count] * inverse) * quarter
        g = jnp.where(hot, g - label, g)
        g0 = jnp.where(lane == 0, g[:, 0:128] - blank, g[:, 0:128])
        grad[start:start + count, 128:] = g[:, 128:].astype(BF16)
        grad[start:start + count, 0:128] = g0.astype(BF16)
        bias_acc[:, 128:] += jnp.sum(g[:, 128:].reshape(count // 8, 8, V - 128), axis=0)
        bias_acc[:, 0:128] += jnp.sum(g0.reshape(count // 8, 8, 128), axis=0)

    beta = bsend[...]
    frame_shift, label_shift = pltpu.roll(beta, 127, 1), pltpu.roll(beta, LB - 1, 0)
    occupancies(frame_shift, label_shift)
    for u in range(LB - 1):
        backward(u, 0, FR - 16)
    arrived("frame")
    arrived("label")
    occupancies(
        jnp.where(lane == FR - 1, brow[:, 0:1], frame_shift),
        jnp.where(label_row == LB - 1, bcol[0:1, :], label_shift),
    )
    for u in range(LB - 1):
        backward(u, FR - 16, 16)
    backward(LB - 1, 0, FR)

    def product(half, q, ref):
        base = pl.multiple_of(half * 512 + q * 256, 256)
        r = lax.dot_general(
            joint[...], grad[:, pl.ds(base, 256)], (((0,), (0,)), ((), ())), preferred_element_type=F32
        )
        ref[q * 1280:q * 1280 + 640] = r[:, 0:128]
        ref[q * 1280 + 640:q * 1280 + 1280] = r[:, 128:256]

    for q in range(2):
        product(other, q, peer_half)
        if q == 0:
            for k in range(8):
                peer_half[HALF + k:HALF + k + 1] = jnp.sum(bias_acc[:, k * 128:(k + 1) * 128], axis=0, keepdims=True)
            acc[HALF:HALF + 8] = peer_half[HALF:HALF + 8]
            send(rows(peer_half, HALF, 8), rows(core_recv, HALF, 8), "bias", sibling)
        for start, size in ((0, 768), (768, 512)):
            part = q * 1280 + start
            send(rows(peer_half, part, size), rows(core_recv, part, size), ("half", part), sibling)
    product(c, 0, acc)

    arrived(("half", A1))
    acc[0:768] += core_recv[0:768]
    for r in far4:
        send(rows(acc, A1 + (x + r) % NX * 192, 192), r1a1.at[r - 1], "a1 1", xp(r))
    arrived("bias")
    arrived(("half", B))
    bias_tile = acc[HALF:HALF + 8] + core_recv[HALF:HALF + 8]
    for k in range(NY):
        send_b[k, 0:64] = acc[B + k * 64:B + k * 64 + 64] + core_recv[B + k * 64:B + k * 64 + 64]
        send_b[k, 64:72] = bias_tile
    for r in far8:
        send(send_b.at[(y + r) % NY], r1b.at[y], "b 1", yp(r))
    product(c, 1, acc)
    arrived(("half", A2))
    acc[A2:C] += core_recv[A2:C]
    for r in far4:
        send(rows(acc, A2 + (x + r) % NX * 192, 192), r1a2.at[r - 1], "a2 1", xp(r))
    arrived(("half", C))
    acc[C:HALF] += core_recv[C:HALF]
    for r in far8:
        send(rows(acc, C + (z + r) % NZ * 64, 64), r1c.at[r - 1], "c 1", zp(r))
    r1b[y] = send_b[y]

    enc_acc[...] = jnp.zeros_like(enc_acc)

    def pre(g, _):
        first = pl.multiple_of(g * ROWS, 128)
        gj = lax.dot_general(
            grad[pl.ds(first, ROWS)], w_ref[...], (((1,), (1,)), ((), ())), preferred_element_type=F32
        )
        j = joint[pl.ds(first, ROWS)].astype(F32)
        gp = gj * (1.0 - j * j)
        enc_acc[0:FR] += (gp[0:FR] + gp[FR:2 * FR]) + (gp[2 * FR:3 * FR] + gp[3 * FR:4 * FR])
        for k in range(GU):
            pred_acc[pl.ds(g * GU + k, 1), 0:H] = jnp.sum(gp[k * FR:(k + 1) * FR], axis=0, keepdims=True)
        return 0

    pred_acc[...] = jnp.zeros_like(pred_acc)
    lax.fori_loop(0, LB // GU, pre, 0)
    for k in range(5):
        enc_t[k * 128:(k + 1) * 128] = jnp.transpose(enc_acc[:, k * 128:(k + 1) * 128])

    def piece(r):
        return rows(enc_t, (z + r) % NZ * 80, 80)

    send(piece(4), e_up.at[0], "e up 0", zp(1))
    wide = pred_acc[...]
    for cc in range(2):
        for xx in range(4):
            for yy in range(4):
                start = (xx * 8 + yy * 2 + cc) * 20
                lo = start // 128 * 128
                two = wide[:, lo:lo + 256]
                pbuf[cc, xx, yy] = pltpu.roll(two, (256 - (start - lo)) % 256, 1)[:, 0:128]
    send(pbuf.at[other], p1_recv, "p 1", sibling)

    arrived("e up 0")
    e_up[0] += piece(3)[...]
    send(e_up.at[0], e_up.at[1], "e up 1", zp(1))
    send(piece(5), e_down.at[0], "e down 0", zp(7))

    arrived("a1 1")
    s1a1[...] = (rows(acc, A1 + x * 192, 192)[...] + r1a1[0]) + (r1a1[1] + r1a1[2])
    for r in far8:
        send(rows(s1a1, (y + r) % NY * 24, 24), r2a1.at[r - 1], "a1 2", yp(r))
    arrived("b 1")
    sum_b = r1b[0]
    for k in range(1, NY):
        sum_b = sum_b + r1b[k]
    for k in range(NZ):
        s2b[k, 0:8] = sum_b[k * 8:k * 8 + 8]
        s2b[k, 8:16] = sum_b[64:72]
    for r in far8:
        send(s2b.at[(z + r) % NZ], r2b.at[z], "b 2", zp(r))
    arrived("a2 1")
    s1a2[...] = (rows(acc, A2 + x * 192, 192)[...] + r1a2[0]) + (r1a2[1] + r1a2[2])
    for r in far8:
        send(rows(s1a2, (z + r) % NZ * 24, 24), r2a2.at[r - 1], "a2 2", zp(r))
    arrived("c 1")
    sum_c = rows(acc, C + z * 64, 64)[...]
    for k in range(7):
        sum_c = sum_c + r1c[k]
    s1c[...] = sum_c
    for r in far8:
        send(rows(s1c, (y + r) % NY * 8, 8), r2c.at[r - 1], "c 2", yp(r))
    r2b[z] = s2b[z]

    arrived("e up 1")
    e_up[1] += piece(2)[...]
    send(e_up.at[1], e_up.at[2], "e up 2", zp(1))
    arrived("e down 0")
    e_down[0] += piece(6)[...]
    send(e_down.at[0], e_down.at[1], "e down 1", zp(7))
    arrived("p 1")
    pbuf[c] = pbuf[c] + p1_recv[...]
    for r in far4:
        send(pbuf.at[c, (x + r) % NX], p2_recv.at[r - 1], "p 2", xp(r))

    before = list(index)

    arrived("b 2")
    sum_b = r2b[0]
    for k in range(1, NZ):
        sum_b = sum_b + r2b[k]
    r3b[x] = sum_b
    for r in far4:
        send(r3b.at[x], r3b.at[x], "b 3", xp(r))
    arrived("a1 2")
    sum_a = rows(s1a1, y * 24, 24)[...]
    for k in range(7):
        sum_a = sum_a + r2a1[k]
    r3a1[z] = sum_a
    for r in far8:
        send(r3a1.at[z], r3a1.at[z], "a1 3", zp(r))
    arrived("a2 2")
    sum_a = rows(s1a2, z * 24, 24)[...]
    for k in range(7):
        sum_a = sum_a + r2a2[k]
    r3a2[y] = sum_a
    for r in far8:
        send(r3a2.at[y], r3a2.at[y], "a2 3", yp(r))
    arrived("c 2")
    sum_c = rows(s1c, y * 8, 8)[...]
    for k in range(7):
        sum_c = sum_c + r2c[k]
    r3c[x] = sum_c
    for r in far4:
        send(r3c.at[x], r3c.at[x], "c 3", xp(r))

    arrived("e up 2")
    e_up[2] += piece(1)[...]
    send(e_up.at[2], e_up.at[3], "e up 3", zp(1))
    arrived("e down 1")
    e_down[1] += piece(7)[...]
    send(e_down.at[1], e_down.at[2], "e down 2", zp(7))
    arrived("p 2")
    pbuf[c, x] = (pbuf[c, x] + p2_recv[0]) + (p2_recv[1] + p2_recv[2])
    for r in far4:
        to = (ylo + r) % 4
        send(pbuf.at[c, x, to], p3_recv.at[r - 1], "p 3", place(x, yhi * 4 + to, z, c))

    base = c * HALF

    def spread(start, size, kind, peer, order, apart=False):
        part = rows(out_ref, base + start, size)
        for r in order:
            send(part, part, (kind, r) if apart else kind, peer(r))

    def across(start, size):
        part = rows(out_ref, base + start, size)
        send(part, part, "core", sibling)

    arrived("b 3")
    sum_b = (r3b[0] + r3b[1]) + (r3b[2] + r3b[3])
    rows(out_ref, base + B + (y * 8 + z) * 8, 8)[...] = sum_b[0:8]
    bias_out[...] = sum_b[8:16]
    spread(B + (y * 8 + z) * 8, 8, "b z", zp, far8)
    arrived("a1 3")
    sum_a = r3a1[0]
    for k in range(1, NZ):
        sum_a = sum_a + r3a1[k]
    rows(out_ref, base + A1 + (x * 8 + y) * 24, 24)[...] = sum_a
    spread(A1 + (x * 8 + y) * 24, 24, "a1 y", yp, far8, True)
    spread(A1 + (x * 8 + y) * 24, 24, "a1 x", xp, far4, True)
    arrived("a2 3")
    sum_a = r3a2[0]
    for k in range(1, NY):
        sum_a = sum_a + r3a2[k]
    rows(out_ref, base + A2 + (x * 8 + z) * 24, 24)[...] = sum_a
    spread(A2 + (x * 8 + z) * 24, 24, "a2 z", zp, far8, True)
    spread(A2 + (x * 8 + z) * 24, 24, "a2 x", xp, far4, True)
    arrived("c 3")
    rows(out_ref, base + C + (z * 8 + y) * 8, 8)[...] = (r3c[0] + r3c[1]) + (r3c[2] + r3c[3])
    spread(C + (z * 8 + y) * 8, 8, "c y", yp, far8)

    arrived("e up 3")
    arrived("e down 2")
    e_sum[...] = piece(0)[...] + (e_up[3] + e_down[2])
    send(rows(e_sum, (1 - yhi) * 40, 40), e_last, "e y", yp(4))
    drain(before)

    for n, r in enumerate(near8):
        arrived(("a1 y", r))
        spread(A1 + (x * 8 + (y + NY - r) % NY) * 24, 24, "a1 x", xp, far4, True)
        arrived(("a2 z", r))
        spread(A2 + (x * 8 + (z + NZ - r) % NZ) * 24, 24, "a2 x", xp, far4, True)
        if n == 3:
            arrived("b z")
            spread(B + y * 64, 64, "b y", yp, far8, True)
            arrived("c y")
            spread(C + z * 64, 64, "c z", zp, far8, True)
    across(A1 + x * 192, 192)
    across(A2 + x * 192, 192)
    across(B + y * 64, 64)
    across(C + z * 64, 64)

    arrived("p 3")
    pred_out[...] = ((pbuf[c, x, ylo] + p3_recv[0]) + (p3_recv[1] + p3_recv[2]))[:, 0:20]

    for r in near8:
        arrived(("b y", r))
        across(B + (y + NY - r) % NY * 64, 64)
        arrived(("c z", r))
        across(C + (z + NZ - r) % NZ * 64, 64)
    for r in near4:
        arrived(("a1 x", r))
        across(A1 + (x + NX - r) % NX * 192, 192)
        arrived(("a2 x", r))
        across(A2 + (x + NX - r) % NX * 192, 192)
    arrived("e y")
    enc_out[...] = (rows(e_sum, yhi * 40, 40)[...] + e_last[...])[:, 0:FR]
    arrived("core")

    drain(list(index))


def finish(weight, bias, enc, pred, weight_out, bias_out, enc_out, pred_out, sem):
    copies = [
        pltpu.make_async_copy(rows(weight, k * H, H), weight_out.at[:, pl.ds(k * 128, 128)], sem.at[k])
        for k in range(8)
    ]
    copies += [
        pltpu.make_async_copy(src, dst, sem.at[8 + k])
        for k, (src, dst) in enumerate(((bias, bias_out), (enc, enc_out), (pred, pred_out)))
    ]
    for copy in copies:
        copy.start()
    for copy in copies:
        copy.wait()


def vm(*shape, dtype=F32):
    return pltpu.VMEM(shape, dtype)


def local(encoder_out, predictor_out, out_weight, out_bias, target_labels, lengths, alpha, beta, log_likelihood):
    vmem = pl.BlockSpec(memory_space=pltpu.VMEM)
    hbm = pl.BlockSpec(memory_space=pltpu.HBM)
    sums = pl.pallas_call(
        kernel,
        out_shape=(vm(2 * HALF, 128), vm(8, 128), vm(40, FR), vm(LB, 20)),
        in_specs=[hbm] * 8 + [pl.BlockSpec(memory_space=pltpu.SMEM)],
        out_specs=(vmem, vmem, vmem, vmem),
        scratch_shapes=[
            vm(FR, H, dtype=BF16), vm(LB, H, dtype=BF16), vm(H, V, dtype=BF16), vm(1, V),
            pltpu.SMEM((LB,), jnp.int32), pltpu.SMEM((2,), jnp.int32), vm(LB, FR), vm(LB, FR),
            pltpu.SemaphoreType.DMA((8,)),
            vm(FR, H), vm(LB, H), vm(FR * LB, H, dtype=BF16), vm(FR * LB, V), vm(FR * LB, V, dtype=BF16),
            vm(LB, 128), vm(LB, 128), vm(8, 128), vm(3, 128, 128), vm(FR, 128), vm(FR, 128), vm(FR, 128), vm(FR, 128), vm(FR, 128),
            vm(FR, 128), vm(FR, 128),
            vm(8, V), vm(HALF + 8, 128), vm(HALF + 8, 128), vm(HALF + 8, 128), vm(8, 72, 128),
            vm(3, 192, 128), vm(8, 72, 128), vm(3, 192, 128), vm(7, 64, 128),
            vm(192, 128), vm(192, 128), vm(64, 128), vm(8, 16, 128),
            vm(7, 24, 128), vm(8, 16, 128), vm(7, 24, 128), vm(7, 8, 128),
            vm(8, 24, 128), vm(4, 16, 128), vm(8, 24, 128), vm(4, 8, 128),
            vm(128, H), vm(H, 128), vm(4, 80, 128), vm(3, 80, 128), vm(80, 128), vm(40, 128),
            vm(LB, 768), vm(2, 4, 4, LB, 128), vm(4, 4, LB, 128), vm(3, 4, LB, 128), vm(3, LB, 128),
            pltpu.SemaphoreType.DMA((SEMS,)), pltpu.SemaphoreType.DMA((SEMS,)),
        ],
        compiler_params=pltpu.CompilerParams(
            collective_id=0, has_side_effects=True, vmem_limit_bytes=44 * 2**20
        ),
        name="joint_backward",
    )(*(
        pltpu.with_memory_space_constraint(a, pltpu.HBM) for a in (
            encoder_out, predictor_out, out_weight, out_bias.reshape(1, V), target_labels, lengths, alpha.T, beta.T,
        )
    ), log_likelihood)
    weight, bias, enc, pred = pl.pallas_call(
        finish,
        out_shape=(
            jax.ShapeDtypeStruct((H, V), F32),
            jax.ShapeDtypeStruct((8, 128), F32),
            jax.ShapeDtypeStruct((40, FR), F32),
            jax.ShapeDtypeStruct((LB, 20), F32),
        ),
        in_specs=[pl.BlockSpec(memory_space=pl.ANY)] * 4,
        out_specs=[hbm] * 4,
        scratch_shapes=[pltpu.SemaphoreType.DMA((11,))],
        compiler_params=pltpu.CompilerParams(vmem_limit_bytes=2 * 2**20),
        name="finish",
    )(*sums)
    return enc.T, pred, weight, bias.reshape(V)


def solution(mesh):
    placed = (
        P("frames", None), P("labels", None), P(), P(), P("labels"), P(),
        P("frames", "labels"), P("frames", "labels"), P(),
    )
    return jax.shard_map(
        local,
        mesh=mesh,
        in_specs=placed,
        out_specs=(P("frames", "labels"), P("labels", "frames"), P(), P()),
        check_vma=False,
    )
```

```python
import jax
import jax.numpy as jnp
from jax import lax
from jax.experimental import pallas as pl
from jax.experimental.pallas import tpu as pltpu
from jax.sharding import PartitionSpec as P

MESH = pl.DeviceIdType.MESH
FR, LB, H, V = 96, 16, 640, 1024
GU = 4
ROWS = FR * GU
NX, NY, NZ = 4, 8, 8
HALF = 2560
A1, B, A2, C = 0, 768, 1280, 2048
SEMS = 80
F32, BF16 = jnp.float32, jnp.bfloat16


def place(x, y, z, c):
    return (x * 8 + (y % 4) * 2 + c, z * 2 + y // 4)


def rows(ref, start, size):
    return ref.at[pl.ds(pl.multiple_of(start, 8), size)]


def kernel(
    enc_in, pred_in, w_in, bias_in, labels_in, lengths_in, alpha_in, beta_in, ll_ref,
    out_ref, bias_out, enc_out, pred_out,
    enc_ref, pred_ref, w_ref, bias_ref, labels_ref, lengths_ref, alpha_ref, beta_ref, isem,
    encf, predf, joint, expo, grad, bsend, brow, bcol, turn, alpha_t, total, ssum, slab, sblank, occb, occl,
    bias_acc, peer_half, core_recv, acc, send_b,
    r1a1, r1b, r1a2, r1c, s1a1, s1a2, s1c, s2b, r2a1, r2b, r2a2, r2c,
    r3a1, r3b, r3a2, r3c,
    enc_acc, enc_t, e_up, e_down, e_sum, e_last, pred_acc, pbuf, p1_recv, p2_recv, p3_recv,
    ssem, rsem,
):
    f = lax.axis_index("frames")
    l = lax.axis_index("labels")
    x, ylo, c = f // 8, (f // 2) % 4, f % 2
    z, yhi = l // 2, l % 2
    y = yhi * 4 + ylo
    other = 1 - c
    sibling = place(x, y, z, other)
    far8, near8, far4, near4 = (4, 3, 5, 2, 6, 1, 7), (1, 7, 2, 6, 3, 5, 4), (2, 1, 3), (1, 3, 2)

    def xp(r):
        return place((x + r) % NX, y, z, c)

    def yp(r):
        return place(x, (y + r) % NY, z, c)

    def zp(r):
        return place(x, y, (z + r) % NZ, c)

    index, amount = {}, {}

    def send(src, dst, kind, to):
        k = index.setdefault(kind, len(index))
        size = 1
        for n in src.shape[:-1]:
            size *= n
        amount[kind] = amount.get(kind, 0) + size
        pltpu.make_async_remote_copy(
            src_ref=src, dst_ref=dst, send_sem=ssem.at[k], recv_sem=rsem.at[k],
            device_id=to, device_id_type=MESH,
        ).start()

    def wait(sem, kind):
        ref = out_ref.at[pl.ds(0, amount[kind])]
        pltpu.make_async_copy(ref, ref, sem.at[index[kind]]).wait()

    def arrived(kind):
        wait(rsem, kind)

    gone = set()

    def drain(kinds):
        for kind in kinds:
            if kind not in gone:
                gone.add(kind)
                wait(ssem, kind)

    loads = [
        pltpu.make_async_copy(src, dst, isem.at[k])
        for k, (src, dst) in enumerate((
            (enc_in, enc_ref), (pred_in, pred_ref), (w_in, w_ref), (beta_in, beta_ref), (alpha_in, alpha_ref),
            (bias_in, bias_ref), (labels_in, labels_ref), (lengths_in, lengths_ref),
        ))
    ]
    for load in loads:
        load.start()

    barrier = pltpu.get_barrier_semaphore()
    peers = [sibling]
    peers += [xp(r) for r in range(1, NX)] + [yp(r) for r in range(1, NY)] + [zp(r) for r in range(1, NZ)]
    peers += [((f + 1) % 32, l), (f, (l + 1) % 16)]
    for p in peers:
        pl.semaphore_signal(barrier, inc=1, device_id=p, device_id_type=MESH)

    lane = lax.broadcasted_iota(jnp.int32, (1, 128), 1)
    vocab = lax.broadcasted_iota(jnp.int32, (1, V), 1)

    def squash(g):
        for k in range(GU):
            u = g * GU + k
            joint[u * FR:(u + 1) * FR] = jnp.tanh(encf[...] + predf[u:u + 1]).astype(BF16)

    def forward(g):
        logits = jnp.dot(joint[g * ROWS:(g + 1) * ROWS], w_ref[...], preferred_element_type=F32) + bias_ref[...]
        for k in range(GU):
            u = g * GU + k
            part = logits[k * FR:(k + 1) * FR]
            e = jnp.exp(part)
            expo[u * FR:(u + 1) * FR] = e
            hot = vocab == labels_ref[u]
            here = lane == u
            ssum[...] = jnp.where(here, jnp.sum(e, axis=1, keepdims=True), ssum[...])
            slab[...] = jnp.where(here, jnp.sum(jnp.where(hot, part, 0.0), axis=1, keepdims=True), slab[...])
            sblank[...] = jnp.where(here, part[:, 0:1], sblank[...])

    loads[0].wait()
    loads[1].wait()
    encf[...] = enc_ref[...].astype(F32)
    predf[...] = pred_ref[...].astype(F32)
    ssum[...] = jnp.ones_like(ssum)
    slab[...] = jnp.zeros_like(slab)
    sblank[...] = jnp.zeros_like(sblank)
    squash(0)
    for load in loads[2:]:
        load.wait()
    bsend[...] = jnp.zeros_like(bsend)
    bsend[:, 0:FR] = beta_ref[...]
    turn[...] = jnp.zeros_like(turn)
    turn[0, 0:LB, 0:FR] = alpha_ref[...]
    squash(1)
    forward(0)
    pl.semaphore_wait(barrier, len(peers))
    send(bsend, brow, "frame", ((f + 31) % 32, l))
    send(bsend.at[pl.ds(0, 8)], bcol, "label", (f, (l + 15) % 16))
    squash(2)
    forward(1)
    squash(3)
    forward(2)
    forward(3)

    frame_len, label_len, log_total = lengths_ref[0], lengths_ref[1], ll_ref[0]
    label_row = lax.broadcasted_iota(jnp.int32, (LB, 128), 0)
    t_pos = lax.broadcasted_iota(jnp.int32, (FR, 128), 0) + f * FR
    u_here = lax.broadcasted_iota(jnp.int32, (FR, 128), 1)
    u_pos = u_here + l * LB
    total[...] = ssum[...]
    ssum[...] = 4.0 / total[...]
    alpha_t[...] = jnp.transpose(turn[0])[0:FR]

    def occupancies(next_frame, next_label):
        turn[1, 0:LB] = next_frame
        turn[2, 0:LB] = next_label
        alpha = alpha_t[...]
        beta_frame = jnp.transpose(turn[1])[0:FR]
        beta_label = jnp.transpose(turn[2])[0:FR]
        lse = jnp.log(total[...])
        inner = (t_pos < frame_len - 1) & (u_pos <= label_len)
        final = (t_pos == frame_len - 1) & (u_pos == label_len)
        blank_ok = (inner | final) & (u_here < LB)
        blank_arg = alpha + (sblank[...] - lse) + jnp.where(inner, beta_frame, 0.0) - log_total
        occb[...] = jnp.where(blank_ok, jnp.exp(jnp.where(blank_ok, blank_arg, 0.0)), 0.0)
        label_ok = (t_pos < frame_len) & (u_pos < label_len) & (u_here < LB)
        label_arg = alpha + (slab[...] - lse) + beta_label - log_total
        occl[...] = jnp.where(label_ok, jnp.exp(jnp.where(label_ok, label_arg, 0.0)), 0.0)

    bias_acc[...] = jnp.zeros_like(bias_acc)

    def backward(u, low, count):
        start = u * FR + low
        blank, label, inverse = (ref[low:low + count, u:u + 1] for ref in (occb, occl, ssum))
        quarter = (blank + label) * 0.25
        hot = vocab == labels_ref[u]
        g = (expo[start:start + count] * inverse) * quarter
        g = jnp.where(hot, g - label, g)
        g0 = jnp.where(lane == 0, g[:, 0:128] - blank, g[:, 0:128])
        grad[start:start + count, 128:] = g[:, 128:].astype(BF16)
        grad[start:start + count, 0:128] = g0.astype(BF16)
        bias_acc[:, 128:] += jnp.sum(g[:, 128:].reshape(count // 8, 8, V - 128), axis=0)
        bias_acc[:, 0:128] += jnp.sum(g0.reshape(count // 8, 8, 128), axis=0)

    beta = bsend[...]
    frame_shift, label_shift = pltpu.roll(beta, 127, 1), pltpu.roll(beta, LB - 1, 0)
    occupancies(frame_shift, label_shift)
    for u in range(LB - 1):
        backward(u, 0, FR - 16)
    arrived("frame")
    arrived("label")
    occupancies(
        jnp.where(lane == FR - 1, brow[:, 0:1], frame_shift),
        jnp.where(label_row == LB - 1, bcol[0:1, :], label_shift),
    )
    for u in range(LB - 1):
        backward(u, FR - 16, 16)
    backward(LB - 1, 0, FR)

    def product(half, q, ref):
        base = pl.multiple_of(half * 512 + q * 256, 256)
        r = lax.dot_general(
            joint[...], grad[:, pl.ds(base, 256)], (((0,), (0,)), ((), ())), preferred_element_type=F32
        )
        ref[q * 1280:q * 1280 + 640] = r[:, 0:128]
        ref[q * 1280 + 640:q * 1280 + 1280] = r[:, 128:256]

    for q in range(2):
        product(other, q, peer_half)
        if q == 0:
            for k in range(8):
                peer_half[HALF + k:HALF + k + 1] = jnp.sum(bias_acc[:, k * 128:(k + 1) * 128], axis=0, keepdims=True)
            acc[HALF:HALF + 8] = peer_half[HALF:HALF + 8]
            send(rows(peer_half, HALF, 8), rows(core_recv, HALF, 8), "bias", sibling)
        for start, size in ((0, 768), (768, 512)):
            part = q * 1280 + start
            send(rows(peer_half, part, size), rows(core_recv, part, size), ("half", part), sibling)
    product(c, 0, acc)

    arrived(("half", A1))
    acc[0:768] += core_recv[0:768]
    for r in far4:
        send(rows(acc, A1 + (x + r) % NX * 192, 192), r1a1.at[r - 1], "a1 1", xp(r))
    arrived("bias")
    arrived(("half", B))
    bias_tile = acc[HALF:HALF + 8] + core_recv[HALF:HALF + 8]
    for k in range(NY):
        send_b[k, 0:64] = acc[B + k * 64:B + k * 64 + 64] + core_recv[B + k * 64:B + k * 64 + 64]
        send_b[k, 64:72] = bias_tile
    for r in far8:
        send(send_b.at[(y + r) % NY], r1b.at[y], "b 1", yp(r))
    product(c, 1, acc)
    arrived(("half", A2))
    acc[A2:C] += core_recv[A2:C]
    for r in far4:
        send(rows(acc, A2 + (x + r) % NX * 192, 192), r1a2.at[r - 1], "a2 1", xp(r))
    arrived(("half", C))
    acc[C:HALF] += core_recv[C:HALF]
    for r in far8:
        send(rows(acc, C + (z + r) % NZ * 64, 64), r1c.at[r - 1], "c 1", zp(r))
    r1b[y] = send_b[y]

    enc_acc[...] = jnp.zeros_like(enc_acc)

    def pre(g, _):
        first = pl.multiple_of(g * ROWS, 128)
        gj = lax.dot_general(
            grad[pl.ds(first, ROWS)], w_ref[...], (((1,), (1,)), ((), ())), preferred_element_type=F32
        )
        j = joint[pl.ds(first, ROWS)].astype(F32)
        gp = gj * (1.0 - j * j)
        enc_acc[0:FR] += (gp[0:FR] + gp[FR:2 * FR]) + (gp[2 * FR:3 * FR] + gp[3 * FR:4 * FR])
        for k in range(GU):
            pred_acc[pl.ds(g * GU + k, 1), 0:H] = jnp.sum(gp[k * FR:(k + 1) * FR], axis=0, keepdims=True)
        return 0

    pred_acc[...] = jnp.zeros_like(pred_acc)
    lax.fori_loop(0, LB // GU, pre, 0)
    for k in range(5):
        enc_t[k * 128:(k + 1) * 128] = jnp.transpose(enc_acc[:, k * 128:(k + 1) * 128])

    def piece(r):
        return rows(enc_t, (z + r) % NZ * 80, 80)

    send(piece(4), e_up.at[0], "e up 0", zp(1))
    wide = pred_acc[...]
    for cc in range(2):
        for xx in range(4):
            for yy in range(4):
                start = (xx * 8 + yy * 2 + cc) * 20
                lo = start // 128 * 128
                two = wide[:, lo:lo + 256]
                pbuf[cc, xx, yy] = pltpu.roll(two, (256 - (start - lo)) % 256, 1)[:, 0:128]
    send(pbuf.at[other], p1_recv, "p 1", sibling)

    arrived("a1 1")
    s1a1[...] = (rows(acc, A1 + x * 192, 192)[...] + r1a1[0]) + (r1a1[1] + r1a1[2])
    for r in far8:
        send(rows(s1a1, (y + r) % NY * 24, 24), r2a1.at[r - 1], "a1 2", yp(r))
    arrived("b 1")
    sum_b = r1b[0]
    for k in range(1, NY):
        sum_b = sum_b + r1b[k]
    for k in range(NX):
        s2b[k, 0:16] = sum_b[k * 16:k * 16 + 16]
        s2b[k, 16:24] = sum_b[64:72]
    for r in far4:
        send(s2b.at[(x + r) % NX], r2b.at[x], "b 2", xp(r))
    r2b[x] = s2b[x]
    arrived("c 1")
    sum_c = rows(acc, C + z * 64, 64)[...]
    for k in range(7):
        sum_c = sum_c + r1c[k]
    s1c[...] = sum_c
    for r in far4:
        send(rows(s1c, (x + r) % NX * 16, 16), r2c.at[r - 1], "c 2", xp(r))
    arrived("p 1")
    pbuf[c] = pbuf[c] + p1_recv[...]
    for r in far4:
        send(pbuf.at[c, (x + r) % NX], p2_recv.at[r - 1], "p 2", xp(r))
    arrived("e up 0")
    e_up[0] += piece(3)[...]
    arrived("a2 1")
    s1a2[...] = (rows(acc, A2 + x * 192, 192)[...] + r1a2[0]) + (r1a2[1] + r1a2[2])
    for r in far8:
        send(rows(s1a2, (z + r) % NZ * 24, 24), r2a2.at[r - 1], "a2 2", zp(r))
    send(e_up.at[0], e_up.at[1], "e up 1", zp(1))
    send(piece(5), e_down.at[0], "e down 0", zp(7))
    before = list(index)

    arrived("b 2")
    r3b[z] = (r2b[0] + r2b[1]) + (r2b[2] + r2b[3])
    for r in far8:
        send(r3b.at[z], r3b.at[z], "b 3", zp(r))
    arrived("c 2")
    r3c[y] = (rows(s1c, x * 16, 16)[...] + r2c[0]) + (r2c[1] + r2c[2])
    for r in far8:
        send(r3c.at[y], r3c.at[y], "c 3", yp(r))
    arrived("a1 2")
    sum_a = rows(s1a1, y * 24, 24)[...]
    for k in range(7):
        sum_a = sum_a + r2a1[k]
    r3a1[z] = sum_a
    for r in far8:
        send(r3a1.at[z], r3a1.at[z], "a1 3", zp(r))
    arrived("e up 1")
    e_up[1] += piece(2)[...]
    send(e_up.at[1], e_up.at[2], "e up 2", zp(1))
    arrived("e down 0")
    e_down[0] += piece(6)[...]
    send(e_down.at[0], e_down.at[1], "e down 1", zp(7))
    arrived("p 2")
    pbuf[c, x] = (pbuf[c, x] + p2_recv[0]) + (p2_recv[1] + p2_recv[2])
    for r in far4:
        to = (ylo + r) % 4
        send(pbuf.at[c, x, to], p3_recv.at[r - 1], "p 3", place(x, yhi * 4 + to, z, c))
    arrived("a2 2")
    sum_a = rows(s1a2, z * 24, 24)[...]
    for k in range(7):
        sum_a = sum_a + r2a2[k]
    r3a2[y] = sum_a
    for r in far8:
        send(r3a2.at[y], r3a2.at[y], "a2 3", yp(r))

    base = c * HALF

    def spread(start, size, kind, peer, order, apart=False):
        part = rows(out_ref, base + start, size)
        for r in order:
            send(part, part, (kind, r) if apart else kind, peer(r))

    def across(start, size):
        part = rows(out_ref, base + start, size)
        send(part, part, "core", sibling)

    arrived("b 3")
    sum_b = r3b[0]
    for k in range(1, NZ):
        sum_b = sum_b + r3b[k]
    rows(out_ref, base + B + (y * 4 + x) * 16, 16)[...] = sum_b[0:16]
    bias_out[...] = sum_b[16:24]
    spread(B + (y * 4 + x) * 16, 16, "b x", xp, far4)
    arrived("c 3")
    sum_c = r3c[0]
    for k in range(1, NY):
        sum_c = sum_c + r3c[k]
    rows(out_ref, base + C + (z * 4 + x) * 16, 16)[...] = sum_c
    spread(C + (z * 4 + x) * 16, 16, "c x", xp, far4)
    arrived("a1 3")
    sum_a = r3a1[0]
    for k in range(1, NZ):
        sum_a = sum_a + r3a1[k]
    rows(out_ref, base + A1 + (x * 8 + y) * 24, 24)[...] = sum_a
    spread(A1 + (x * 8 + y) * 24, 24, "a1 y", yp, far8, True)
    spread(A1 + (x * 8 + y) * 24, 24, "a1 x", xp, far4, True)
    arrived("e up 2")
    e_up[2] += piece(1)[...]
    send(e_up.at[2], e_up.at[3], "e up 3", zp(1))
    arrived("e down 1")
    e_down[1] += piece(7)[...]
    send(e_down.at[1], e_down.at[2], "e down 2", zp(7))
    drain(before)
    arrived("a2 3")
    sum_a = r3a2[0]
    for k in range(1, NY):
        sum_a = sum_a + r3a2[k]
    rows(out_ref, base + A2 + (x * 8 + z) * 24, 24)[...] = sum_a
    spread(A2 + (x * 8 + z) * 24, 24, "a2 z", zp, far8, True)
    spread(A2 + (x * 8 + z) * 24, 24, "a2 x", xp, far4, True)

    def pass_a1(r):
        arrived(("a1 y", r))
        spread(A1 + (x * 8 + (y + NY - r) % NY) * 24, 24, "a1 x", xp, far4, True)

    def pass_a2(r):
        arrived(("a2 z", r))
        spread(A2 + (x * 8 + (z + NZ - r) % NZ) * 24, 24, "a2 x", xp, far4, True)

    arrived("b x")
    spread(B + y * 64, 64, "b y", yp, far8, True)
    arrived("c x")
    spread(C + z * 64, 64, "c z", zp, far8, True)
    for r in near8:
        pass_a1(r)
    across(A1 + x * 192, 192)
    across(B + y * 64, 64)
    across(C + z * 64, 64)
    arrived("e up 3")
    arrived("e down 2")
    e_sum[...] = piece(0)[...] + (e_up[3] + e_down[2])
    send(rows(e_sum, (1 - yhi) * 40, 40), e_last, "e y", yp(4))
    for r in near8:
        pass_a2(r)
    across(A2 + x * 192, 192)
    arrived("p 3")
    pred_out[...] = ((pbuf[c, x, ylo] + p3_recv[0]) + (p3_recv[1] + p3_recv[2]))[:, 0:20]

    for r in near4:
        arrived(("a1 x", r))
        across(A1 + (x + NX - r) % NX * 192, 192)
    arrived("e y")
    enc_out[...] = (rows(e_sum, yhi * 40, 40)[...] + e_last[...])[:, 0:FR]
    for r in near8:
        arrived(("b y", r))
        across(B + (y + NY - r) % NY * 64, 64)
        arrived(("c z", r))
        across(C + (z + NZ - r) % NZ * 64, 64)
    for r in near4:
        arrived(("a2 x", r))
        across(A2 + (x + NX - r) % NX * 192, 192)
    arrived("core")

    drain(list(index))


def finish(weight, bias, enc, pred, weight_out, bias_out, enc_out, pred_out, sem):
    copies = [
        pltpu.make_async_copy(rows(weight, k * H, H), weight_out.at[:, pl.ds(k * 128, 128)], sem.at[k])
        for k in range(8)
    ]
    copies += [
        pltpu.make_async_copy(src, dst, sem.at[8 + k])
        for k, (src, dst) in enumerate(((bias, bias_out), (enc, enc_out), (pred, pred_out)))
    ]
    for copy in copies:
        copy.start()
    for copy in copies:
        copy.wait()


def vm(*shape, dtype=F32):
    return pltpu.VMEM(shape, dtype)


def local(encoder_out, predictor_out, out_weight, out_bias, target_labels, lengths, alpha, beta, log_likelihood):
    vmem = pl.BlockSpec(memory_space=pltpu.VMEM)
    hbm = pl.BlockSpec(memory_space=pltpu.HBM)
    sums = pl.pallas_call(
        kernel,
        out_shape=(vm(2 * HALF, 128), vm(8, 128), vm(40, FR), vm(LB, 20)),
        in_specs=[hbm] * 8 + [pl.BlockSpec(memory_space=pltpu.SMEM)],
        out_specs=(vmem, vmem, vmem, vmem),
        scratch_shapes=[
            vm(FR, H, dtype=BF16), vm(LB, H, dtype=BF16), vm(H, V, dtype=BF16), vm(1, V),
            pltpu.SMEM((LB,), jnp.int32), pltpu.SMEM((2,), jnp.int32), vm(LB, FR), vm(LB, FR),
            pltpu.SemaphoreType.DMA((8,)),
            vm(FR, H), vm(LB, H), vm(FR * LB, H, dtype=BF16), vm(FR * LB, V), vm(FR * LB, V, dtype=BF16),
            vm(LB, 128), vm(LB, 128), vm(8, 128), vm(3, 128, 128), vm(FR, 128), vm(FR, 128), vm(FR, 128), vm(FR, 128), vm(FR, 128),
            vm(FR, 128), vm(FR, 128),
            vm(8, V), vm(HALF + 8, 128), vm(HALF + 8, 128), vm(HALF + 8, 128), vm(8, 72, 128),
            vm(3, 192, 128), vm(8, 72, 128), vm(3, 192, 128), vm(7, 64, 128),
            vm(192, 128), vm(192, 128), vm(64, 128), vm(4, 24, 128),
            vm(7, 24, 128), vm(4, 24, 128), vm(7, 24, 128), vm(3, 16, 128),
            vm(8, 24, 128), vm(8, 24, 128), vm(8, 24, 128), vm(8, 16, 128),
            vm(128, H), vm(H, 128), vm(4, 80, 128), vm(3, 80, 128), vm(80, 128), vm(40, 128),
            vm(LB, 768), vm(2, 4, 4, LB, 128), vm(4, 4, LB, 128), vm(3, 4, LB, 128), vm(3, LB, 128),
            pltpu.SemaphoreType.DMA((SEMS,)), pltpu.SemaphoreType.DMA((SEMS,)),
        ],
        compiler_params=pltpu.CompilerParams(
            collective_id=0, has_side_effects=True, vmem_limit_bytes=44 * 2**20
        ),
        name="joint_backward",
    )(*(
        pltpu.with_memory_space_constraint(a, pltpu.HBM) for a in (
            encoder_out, predictor_out, out_weight, out_bias.reshape(1, V), target_labels, lengths, alpha.T, beta.T,
        )
    ), log_likelihood)
    weight, bias, enc, pred = pl.pallas_call(
        finish,
        out_shape=(
            jax.ShapeDtypeStruct((H, V), F32),
            jax.ShapeDtypeStruct((8, 128), F32),
            jax.ShapeDtypeStruct((40, FR), F32),
            jax.ShapeDtypeStruct((LB, 20), F32),
        ),
        in_specs=[pl.BlockSpec(memory_space=pl.ANY)] * 4,
        out_specs=[hbm] * 4,
        scratch_shapes=[pltpu.SemaphoreType.DMA((11,))],
        compiler_params=pltpu.CompilerParams(vmem_limit_bytes=2 * 2**20),
        name="finish",
    )(*sums)
    return enc.T, pred, weight, bias.reshape(V)


def solution(mesh):
    placed = (
        P("frames", None), P("labels", None), P(), P(), P("labels"), P(),
        P("frames", "labels"), P("frames", "labels"), P(),
    )
    return jax.shard_map(
        local,
        mesh=mesh,
        in_specs=placed,
        out_specs=(P("frames", "labels"), P("labels", "frames"), P(), P()),
        check_vma=False,
    )
```

```python
import jax
import jax.numpy as jnp
from jax import lax
from jax.experimental import pallas as pl
from jax.experimental.pallas import tpu as pltpu
from jax.sharding import PartitionSpec as P

MESH = pl.DeviceIdType.MESH
FR, LB, H, V = 96, 16, 640, 1024
GU = 4
ROWS = FR * GU
NX, NY, NZ = 4, 8, 8
HALF = 2560
A1, B, A2, C = 0, 768, 1280, 2048
SEMS = 80
F32, BF16 = jnp.float32, jnp.bfloat16


def place(x, y, z, c):
    return (x * 8 + (y % 4) * 2 + c, z * 2 + y // 4)


def rows(ref, start, size):
    return ref.at[pl.ds(pl.multiple_of(start, 8), size)]


def kernel(
    enc_in, pred_in, w_in, bias_in, labels_in, lengths_in, alpha_in, beta_in, ll_ref,
    out_ref, bias_out, enc_out, pred_out,
    enc_ref, pred_ref, w_ref, bias_ref, labels_ref, lengths_ref, alpha_ref, beta_ref, isem,
    encf, predf, joint, expo, grad, bsend, brow, bcol, turn, alpha_t, total, ssum, slab, sblank, occb, occl,
    bias_acc, peer_half, core_recv, acc, send_b,
    r1a1, r1b, r1a2, r1c, s1a1, s1a2, s1c, s2b, r2a1, r2b, r2a2, r2c,
    r3a1, r3b, r3a2, r3c,
    enc_acc, enc_t, e_up, e_down, e_sum, e_last, pred_acc, pbuf, p1_recv, p2_recv, p3_recv,
    ssem, rsem,
):
    f = lax.axis_index("frames")
    l = lax.axis_index("labels")
    x, ylo, c = f // 8, (f // 2) % 4, f % 2
    z, yhi = l // 2, l % 2
    y = yhi * 4 + ylo
    other = 1 - c
    sibling = place(x, y, z, other)
    far8, near8, far4, near4 = (4, 3, 5, 2, 6, 1, 7), (1, 7, 2, 6, 3, 5, 4), (2, 1, 3), (1, 3, 2)

    def xp(r):
        return place((x + r) % NX, y, z, c)

    def yp(r):
        return place(x, (y + r) % NY, z, c)

    def zp(r):
        return place(x, y, (z + r) % NZ, c)

    index, amount = {}, {}

    def send(src, dst, kind, to):
        k = index.setdefault(kind, len(index))
        size = 1
        for n in src.shape[:-1]:
            size *= n
        amount[kind] = amount.get(kind, 0) + size
        pltpu.make_async_remote_copy(
            src_ref=src, dst_ref=dst, send_sem=ssem.at[k], recv_sem=rsem.at[k],
            device_id=to, device_id_type=MESH,
        ).start()

    def wait(sem, kind):
        ref = out_ref.at[pl.ds(0, amount[kind])]
        pltpu.make_async_copy(ref, ref, sem.at[index[kind]]).wait()

    def arrived(kind):
        wait(rsem, kind)

    gone = set()

    def drain(kinds):
        for kind in kinds:
            if kind not in gone:
                gone.add(kind)
                wait(ssem, kind)

    loads = [
        pltpu.make_async_copy(src, dst, isem.at[k])
        for k, (src, dst) in enumerate((
            (enc_in, enc_ref), (pred_in, pred_ref), (w_in, w_ref), (beta_in, beta_ref), (alpha_in, alpha_ref),
            (bias_in, bias_ref), (labels_in, labels_ref), (lengths_in, lengths_ref),
        ))
    ]
    for load in loads:
        load.start()

    barrier = pltpu.get_barrier_semaphore()
    peers = [sibling]
    peers += [xp(r) for r in range(1, NX)] + [yp(r) for r in range(1, NY)] + [zp(r) for r in range(1, NZ)]
    peers += [((f + 1) % 32, l), (f, (l + 1) % 16)]
    for p in peers:
        pl.semaphore_signal(barrier, inc=1, device_id=p, device_id_type=MESH)

    lane = lax.broadcasted_iota(jnp.int32, (1, 128), 1)
    vocab = lax.broadcasted_iota(jnp.int32, (1, V), 1)

    def squash(g):
        for k in range(GU):
            u = g * GU + k
            joint[u * FR:(u + 1) * FR] = jnp.tanh(encf[...] + predf[u:u + 1]).astype(BF16)

    def forward(g):
        logits = jnp.dot(joint[g * ROWS:(g + 1) * ROWS], w_ref[...], preferred_element_type=F32) + bias_ref[...]
        for k in range(GU):
            u = g * GU + k
            part = logits[k * FR:(k + 1) * FR]
            e = jnp.exp(part)
            expo[u * FR:(u + 1) * FR] = e
            hot = vocab == labels_ref[u]
            here = lane == u
            ssum[...] = jnp.where(here, jnp.sum(e, axis=1, keepdims=True), ssum[...])
            slab[...] = jnp.where(here, jnp.sum(jnp.where(hot, part, 0.0), axis=1, keepdims=True), slab[...])
            sblank[...] = jnp.where(here, part[:, 0:1], sblank[...])

    loads[0].wait()
    loads[1].wait()
    encf[...] = enc_ref[...].astype(F32)
    predf[...] = pred_ref[...].astype(F32)
    ssum[...] = jnp.ones_like(ssum)
    slab[...] = jnp.zeros_like(slab)
    sblank[...] = jnp.zeros_like(sblank)
    squash(0)
    for load in loads[2:]:
        load.wait()
    bsend[...] = jnp.zeros_like(bsend)
    bsend[:, 0:FR] = beta_ref[...]
    turn[...] = jnp.zeros_like(turn)
    turn[0, 0:LB, 0:FR] = alpha_ref[...]
    squash(1)
    forward(0)
    pl.semaphore_wait(barrier, len(peers))
    send(bsend, brow, "frame", ((f + 31) % 32, l))
    send(bsend.at[pl.ds(0, 8)], bcol, "label", (f, (l + 15) % 16))
    squash(2)
    forward(1)
    squash(3)
    forward(2)
    forward(3)

    frame_len, label_len, log_total = lengths_ref[0], lengths_ref[1], ll_ref[0]
    label_row = lax.broadcasted_iota(jnp.int32, (LB, 128), 0)
    t_pos = lax.broadcasted_iota(jnp.int32, (FR, 128), 0) + f * FR
    u_here = lax.broadcasted_iota(jnp.int32, (FR, 128), 1)
    u_pos = u_here + l * LB
    total[...] = ssum[...]
    ssum[...] = 4.0 / total[...]
    alpha_t[...] = jnp.transpose(turn[0])[0:FR]

    def occupancies(next_frame, next_label):
        turn[1, 0:LB] = next_frame
        turn[2, 0:LB] = next_label
        alpha = alpha_t[...]
        beta_frame = jnp.transpose(turn[1])[0:FR]
        beta_label = jnp.transpose(turn[2])[0:FR]
        lse = jnp.log(total[...])
        inner = (t_pos < frame_len - 1) & (u_pos <= label_len)
        final = (t_pos == frame_len - 1) & (u_pos == label_len)
        blank_ok = (inner | final) & (u_here < LB)
        blank_arg = alpha + (sblank[...] - lse) + jnp.where(inner, beta_frame, 0.0) - log_total
        occb[...] = jnp.where(blank_ok, jnp.exp(jnp.where(blank_ok, blank_arg, 0.0)), 0.0)
        label_ok = (t_pos < frame_len) & (u_pos < label_len) & (u_here < LB)
        label_arg = alpha + (slab[...] - lse) + beta_label - log_total
        occl[...] = jnp.where(label_ok, jnp.exp(jnp.where(label_ok, label_arg, 0.0)), 0.0)

    bias_acc[...] = jnp.zeros_like(bias_acc)

    def backward(u, low, count):
        start = u * FR + low
        blank, label, inverse = (ref[low:low + count, u:u + 1] for ref in (occb, occl, ssum))
        quarter = (blank + label) * 0.25
        hot = vocab == labels_ref[u]
        g = (expo[start:start + count] * inverse) * quarter
        g = jnp.where(hot, g - label, g)
        g0 = jnp.where(lane == 0, g[:, 0:128] - blank, g[:, 0:128])
        grad[start:start + count, 128:] = g[:, 128:].astype(BF16)
        grad[start:start + count, 0:128] = g0.astype(BF16)
        bias_acc[:, 128:] += jnp.sum(g[:, 128:].reshape(count // 8, 8, V - 128), axis=0)
        bias_acc[:, 0:128] += jnp.sum(g0.reshape(count // 8, 8, 128), axis=0)

    beta = bsend[...]
    frame_shift, label_shift = pltpu.roll(beta, 127, 1), pltpu.roll(beta, LB - 1, 0)
    occupancies(frame_shift, label_shift)
    for u in range(LB - 1):
        backward(u, 0, FR - 16)
    arrived("frame")
    arrived("label")
    occupancies(
        jnp.where(lane == FR - 1, brow[:, 0:1], frame_shift),
        jnp.where(label_row == LB - 1, bcol[0:1, :], label_shift),
    )
    for u in range(LB - 1):
        backward(u, FR - 16, 16)
    backward(LB - 1, 0, FR)

    def product(half, q, ref):
        base = pl.multiple_of(half * 512 + q * 256, 256)
        r = lax.dot_general(
            joint[...], grad[:, pl.ds(base, 256)], (((0,), (0,)), ((), ())), preferred_element_type=F32
        )
        ref[q * 1280:q * 1280 + 640] = r[:, 0:128]
        ref[q * 1280 + 640:q * 1280 + 1280] = r[:, 128:256]

    for q in range(2):
        product(other, q, peer_half)
        for start, size in ((0, 768), (768, 512)):
            part = q * 1280 + start
            send(rows(peer_half, part, size), rows(core_recv, part, size), ("half", part), sibling)
        if q == 0:
            for k in range(8):
                peer_half[HALF + k:HALF + k + 1] = jnp.sum(bias_acc[:, k * 128:(k + 1) * 128], axis=0, keepdims=True)
            acc[HALF:HALF + 8] = peer_half[HALF:HALF + 8]
            send(rows(peer_half, HALF, 8), rows(core_recv, HALF, 8), "bias", sibling)
    product(c, 0, acc)

    arrived(("half", A1))
    acc[0:768] += core_recv[0:768]
    for r in far4:
        send(rows(acc, A1 + (x + r) % NX * 192, 192), r1a1.at[r - 1], "a1 1", xp(r))
    arrived("bias")
    arrived(("half", B))
    bias_tile = acc[HALF:HALF + 8] + core_recv[HALF:HALF + 8]
    for k in range(NY):
        send_b[k, 0:64] = acc[B + k * 64:B + k * 64 + 64] + core_recv[B + k * 64:B + k * 64 + 64]
        send_b[k, 64:72] = bias_tile
    for r in far8:
        send(send_b.at[(y + r) % NY], r1b.at[y], "b 1", yp(r))
    product(c, 1, acc)
    arrived(("half", A2))
    acc[A2:C] += core_recv[A2:C]
    for r in far4:
        send(rows(acc, A2 + (x + r) % NX * 192, 192), r1a2.at[r - 1], "a2 1", xp(r))
    arrived(("half", C))
    acc[C:HALF] += core_recv[C:HALF]
    for r in far8:
        send(rows(acc, C + (z + r) % NZ * 64, 64), r1c.at[r - 1], "c 1", zp(r))
    r1b[y] = send_b[y]

    enc_acc[...] = jnp.zeros_like(enc_acc)

    def pre(g, _):
        first = pl.multiple_of(g * ROWS, 128)
        gj = lax.dot_general(
            grad[pl.ds(first, ROWS)], w_ref[...], (((1,), (1,)), ((), ())), preferred_element_type=F32
        )
        j = joint[pl.ds(first, ROWS)].astype(F32)
        gp = gj * (1.0 - j * j)
        enc_acc[0:FR] += (gp[0:FR] + gp[FR:2 * FR]) + (gp[2 * FR:3 * FR] + gp[3 * FR:4 * FR])
        for k in range(GU):
            pred_acc[pl.ds(g * GU + k, 1), 0:H] = jnp.sum(gp[k * FR:(k + 1) * FR], axis=0, keepdims=True)
        return 0

    pred_acc[...] = jnp.zeros_like(pred_acc)
    lax.fori_loop(0, LB // GU, pre, 0)
    for k in range(5):
        enc_t[k * 128:(k + 1) * 128] = jnp.transpose(enc_acc[:, k * 128:(k + 1) * 128])

    def piece(r):
        return rows(enc_t, (z + r) % NZ * 80, 80)

    send(piece(4), e_up.at[0], "e up 0", zp(1))
    wide = pred_acc[...]
    for cc in range(2):
        for xx in range(4):
            for yy in range(4):
                start = (xx * 8 + yy * 2 + cc) * 20
                lo = start // 128 * 128
                two = wide[:, lo:lo + 256]
                pbuf[cc, xx, yy] = pltpu.roll(two, (256 - (start - lo)) % 256, 1)[:, 0:128]
    send(pbuf.at[other], p1_recv, "p 1", sibling)

    arrived("a1 1")
    s1a1[...] = (rows(acc, A1 + x * 192, 192)[...] + r1a1[0]) + (r1a1[1] + r1a1[2])
    for r in far8:
        send(rows(s1a1, (y + r) % NY * 24, 24), r2a1.at[r - 1], "a1 2", yp(r))
    arrived("b 1")
    sum_b = r1b[0]
    for k in range(1, NY):
        sum_b = sum_b + r1b[k]
    for k in range(NX):
        s2b[k, 0:16] = sum_b[k * 16:k * 16 + 16]
        s2b[k, 16:24] = sum_b[64:72]
    for r in far4:
        send(s2b.at[(x + r) % NX], r2b.at[x], "b 2", xp(r))
    r2b[x] = s2b[x]
    arrived("c 1")
    sum_c = rows(acc, C + z * 64, 64)[...]
    for k in range(7):
        sum_c = sum_c + r1c[k]
    s1c[...] = sum_c
    for r in far4:
        send(rows(s1c, (x + r) % NX * 16, 16), r2c.at[r - 1], "c 2", xp(r))
    arrived("p 1")
    pbuf[c] = pbuf[c] + p1_recv[...]
    for r in far4:
        send(pbuf.at[c, (x + r) % NX], p2_recv.at[r - 1], "p 2", xp(r))
    arrived("e up 0")
    e_up[0] += piece(3)[...]
    arrived("a2 1")
    s1a2[...] = (rows(acc, A2 + x * 192, 192)[...] + r1a2[0]) + (r1a2[1] + r1a2[2])
    for r in far8:
        send(rows(s1a2, (z + r) % NZ * 24, 24), r2a2.at[r - 1], "a2 2", zp(r))
    send(e_up.at[0], e_up.at[1], "e up 1", zp(1))
    send(piece(5), e_down.at[0], "e down 0", zp(7))
    before = list(index)

    arrived("b 2")
    r3b[z] = (r2b[0] + r2b[1]) + (r2b[2] + r2b[3])
    for r in far8:
        send(r3b.at[z], r3b.at[z], "b 3", zp(r))
    arrived("c 2")
    r3c[y] = (rows(s1c, x * 16, 16)[...] + r2c[0]) + (r2c[1] + r2c[2])
    for r in far8:
        send(r3c.at[y], r3c.at[y], "c 3", yp(r))
    arrived("a1 2")
    sum_a = rows(s1a1, y * 24, 24)[...]
    for k in range(7):
        sum_a = sum_a + r2a1[k]
    r3a1[z] = sum_a
    for r in far8:
        send(r3a1.at[z], r3a1.at[z], "a1 3", zp(r))
    arrived("e up 1")
    e_up[1] += piece(2)[...]
    send(e_up.at[1], e_up.at[2], "e up 2", zp(1))
    arrived("e down 0")
    e_down[0] += piece(6)[...]
    send(e_down.at[0], e_down.at[1], "e down 1", zp(7))
    arrived("p 2")
    pbuf[c, x] = (pbuf[c, x] + p2_recv[0]) + (p2_recv[1] + p2_recv[2])
    for r in far4:
        to = (ylo + r) % 4
        send(pbuf.at[c, x, to], p3_recv.at[r - 1], "p 3", place(x, yhi * 4 + to, z, c))
    arrived("a2 2")
    sum_a = rows(s1a2, z * 24, 24)[...]
    for k in range(7):
        sum_a = sum_a + r2a2[k]
    r3a2[y] = sum_a
    for r in far8:
        send(r3a2.at[y], r3a2.at[y], "a2 3", yp(r))

    base = c * HALF

    def spread(start, size, kind, peer, order, apart=False):
        part = rows(out_ref, base + start, size)
        for r in order:
            send(part, part, (kind, r) if apart else kind, peer(r))

    def across(start, size):
        part = rows(out_ref, base + start, size)
        send(part, part, "core", sibling)

    arrived("b 3")
    sum_b = r3b[0]
    for k in range(1, NZ):
        sum_b = sum_b + r3b[k]
    rows(out_ref, base + B + (y * 4 + x) * 16, 16)[...] = sum_b[0:16]
    bias_out[...] = sum_b[16:24]
    spread(B + (y * 4 + x) * 16, 16, "b x", xp, far4)
    arrived("c 3")
    sum_c = r3c[0]
    for k in range(1, NY):
        sum_c = sum_c + r3c[k]
    rows(out_ref, base + C + (z * 4 + x) * 16, 16)[...] = sum_c
    spread(C + (z * 4 + x) * 16, 16, "c x", xp, far4)
    arrived("a1 3")
    sum_a = r3a1[0]
    for k in range(1, NZ):
        sum_a = sum_a + r3a1[k]
    rows(out_ref, base + A1 + (x * 8 + y) * 24, 24)[...] = sum_a
    spread(A1 + (x * 8 + y) * 24, 24, "a1 y", yp, far8, True)
    spread(A1 + (x * 8 + y) * 24, 24, "a1 x", xp, far4, True)
    arrived("e up 2")
    e_up[2] += piece(1)[...]
    send(e_up.at[2], e_up.at[3], "e up 3", zp(1))
    arrived("e down 1")
    e_down[1] += piece(7)[...]
    send(e_down.at[1], e_down.at[2], "e down 2", zp(7))
    drain(before)
    arrived("a2 3")
    sum_a = r3a2[0]
    for k in range(1, NY):
        sum_a = sum_a + r3a2[k]
    rows(out_ref, base + A2 + (x * 8 + z) * 24, 24)[...] = sum_a
    spread(A2 + (x * 8 + z) * 24, 24, "a2 z", zp, far8, True)
    spread(A2 + (x * 8 + z) * 24, 24, "a2 x", xp, far4, True)

    def pass_a1(r):
        arrived(("a1 y", r))
        spread(A1 + (x * 8 + (y + NY - r) % NY) * 24, 24, "a1 x", xp, far4, True)

    def pass_a2(r):
        arrived(("a2 z", r))
        spread(A2 + (x * 8 + (z + NZ - r) % NZ) * 24, 24, "a2 x", xp, far4, True)

    arrived("b x")
    spread(B + y * 64, 64, "b y", yp, far8, True)
    arrived("c x")
    spread(C + z * 64, 64, "c z", zp, far8, True)
    for r in near8:
        pass_a1(r)
    across(A1 + x * 192, 192)
    across(B + y * 64, 64)
    across(C + z * 64, 64)
    arrived("e up 3")
    arrived("e down 2")
    e_sum[...] = piece(0)[...] + (e_up[3] + e_down[2])
    send(rows(e_sum, (1 - yhi) * 40, 40), e_last, "e y", yp(4))
    for r in near8:
        pass_a2(r)
    across(A2 + x * 192, 192)
    arrived("p 3")
    pred_out[...] = ((pbuf[c, x, ylo] + p3_recv[0]) + (p3_recv[1] + p3_recv[2]))[:, 0:20]

    for r in near4:
        arrived(("a1 x", r))
        across(A1 + (x + NX - r) % NX * 192, 192)
    arrived("e y")
    enc_out[...] = (rows(e_sum, yhi * 40, 40)[...] + e_last[...])[:, 0:FR]
    for r in near8:
        arrived(("b y", r))
        across(B + (y + NY - r) % NY * 64, 64)
        arrived(("c z", r))
        across(C + (z + NZ - r) % NZ * 64, 64)
    for r in near4:
        arrived(("a2 x", r))
        across(A2 + (x + NX - r) % NX * 192, 192)
    arrived("core")

    drain(list(index))


def finish(weight, bias, enc, pred, weight_out, bias_out, enc_out, pred_out, sem):
    copies = [
        pltpu.make_async_copy(rows(weight, k * H, H), weight_out.at[:, pl.ds(k * 128, 128)], sem.at[k])
        for k in range(8)
    ]
    copies += [
        pltpu.make_async_copy(src, dst, sem.at[8 + k])
        for k, (src, dst) in enumerate(((bias, bias_out), (enc, enc_out), (pred, pred_out)))
    ]
    for copy in copies:
        copy.start()
    for copy in copies:
        copy.wait()


def vm(*shape, dtype=F32):
    return pltpu.VMEM(shape, dtype)


def local(encoder_out, predictor_out, out_weight, out_bias, target_labels, lengths, alpha, beta, log_likelihood):
    vmem = pl.BlockSpec(memory_space=pltpu.VMEM)
    hbm = pl.BlockSpec(memory_space=pltpu.HBM)
    sums = pl.pallas_call(
        kernel,
        out_shape=(vm(2 * HALF, 128), vm(8, 128), vm(40, FR), vm(LB, 20)),
        in_specs=[hbm] * 8 + [pl.BlockSpec(memory_space=pltpu.SMEM)],
        out_specs=(vmem, vmem, vmem, vmem),
        scratch_shapes=[
            vm(FR, H, dtype=BF16), vm(LB, H, dtype=BF16), vm(H, V, dtype=BF16), vm(1, V),
            pltpu.SMEM((LB,), jnp.int32), pltpu.SMEM((2,), jnp.int32), vm(LB, FR), vm(LB, FR),
            pltpu.SemaphoreType.DMA((8,)),
            vm(FR, H), vm(LB, H), vm(FR * LB, H, dtype=BF16), vm(FR * LB, V), vm(FR * LB, V, dtype=BF16),
            vm(LB, 128), vm(LB, 128), vm(8, 128), vm(3, 128, 128), vm(FR, 128), vm(FR, 128), vm(FR, 128), vm(FR, 128), vm(FR, 128),
            vm(FR, 128), vm(FR, 128),
            vm(8, V), vm(HALF + 8, 128), vm(HALF + 8, 128), vm(HALF + 8, 128), vm(8, 72, 128),
            vm(3, 192, 128), vm(8, 72, 128), vm(3, 192, 128), vm(7, 64, 128),
            vm(192, 128), vm(192, 128), vm(64, 128), vm(4, 24, 128),
            vm(7, 24, 128), vm(4, 24, 128), vm(7, 24, 128), vm(3, 16, 128),
            vm(8, 24, 128), vm(8, 24, 128), vm(8, 24, 128), vm(8, 16, 128),
            vm(128, H), vm(H, 128), vm(4, 80, 128), vm(3, 80, 128), vm(80, 128), vm(40, 128),
            vm(LB, 768), vm(2, 4, 4, LB, 128), vm(4, 4, LB, 128), vm(3, 4, LB, 128), vm(3, LB, 128),
            pltpu.SemaphoreType.DMA((SEMS,)), pltpu.SemaphoreType.DMA((SEMS,)),
        ],
        compiler_params=pltpu.CompilerParams(
            collective_id=0, has_side_effects=True, vmem_limit_bytes=44 * 2**20
        ),
        name="joint_backward",
    )(*(
        pltpu.with_memory_space_constraint(a, pltpu.HBM) for a in (
            encoder_out, predictor_out, out_weight, out_bias.reshape(1, V), target_labels, lengths, alpha.T, beta.T,
        )
    ), log_likelihood)
    weight, bias, enc, pred = pl.pallas_call(
        finish,
        out_shape=(
            jax.ShapeDtypeStruct((H, V), F32),
            jax.ShapeDtypeStruct((8, 128), F32),
            jax.ShapeDtypeStruct((40, FR), F32),
            jax.ShapeDtypeStruct((LB, 20), F32),
        ),
        in_specs=[pl.BlockSpec(memory_space=pl.ANY)] * 4,
        out_specs=[hbm] * 4,
        scratch_shapes=[pltpu.SemaphoreType.DMA((11,))],
        compiler_params=pltpu.CompilerParams(vmem_limit_bytes=2 * 2**20),
        name="finish",
    )(*sums)
    return enc.T, pred, weight, bias.reshape(V)


def solution(mesh):
    placed = (
        P("frames", None), P("labels", None), P(), P(), P("labels"), P(),
        P("frames", "labels"), P("frames", "labels"), P(),
    )
    return jax.shard_map(
        local,
        mesh=mesh,
        in_specs=placed,
        out_specs=(P("frames", "labels"), P("labels", "frames"), P(), P()),
        check_vma=False,
    )
```
